128 devices in a mesh: ctx: 16 (over z_lo, x, core), ch: 8 (over z_hi, y).
Axes of the slice: x: 4, y: 4, z: 4 (z_hi: 2, z_lo: 2; z = z_hi * 2 + z_lo), core: 2. Of those that a mesh axis runs over, the one named last changes fastest.
Arguments:
- signal: bfloat16 [128, 262144], P('ch', 'ctx'), may hold values from -6 to 6
- gate: bfloat16 [128, 262144], P('ch', 'ctx'), may hold values from -6 to 6
- cotangent: bfloat16 [128, 262144], P('ch', 'ctx'), may hold values from -6 to 6
- skip_gain: float32 [128], P('ch'), may hold values from 0.5 to 1.5
- filter_taps: float32 [16, 262144], P(None, 'ctx'), may hold values from -0.01171875 to 0.01171875
Outputs:
- output: bfloat16 [128, 262144], P('ch', 'ctx')
- grad_gate: bfloat16 [128, 262144], P('ch', 'ctx')
- grad_signal: bfloat16 [128, 262144], P('ch', 'ctx')
- grad_taps: float32 [16, 262144], P('ch', 'ctx')
The draws below stay inside these ranges and needn't reach their ends.
All inputs are finite; a program needn't handle non-finite values.
Results may differ from the reference program's by a relative error of at most 0.017.
Values may be sent and summed in bfloat16 or wider, within the bound.
A program may use at most 128 MiB of HBM per device.

```python
import math
import jax
import jax.numpy as jnp
from jax import lax

N1 = 1024
N2 = 512
CHAN_DEV = 16
SEQ = 262144
CHANNELS = 128
N_CH = 8


def level_of(own_key, extent, split, low, high):
    def one(axis_at, shards_of):
        steps = jax.random.uniform(jax.random.fold_in(jax.random.fold_in(own_key, 6), axis_at), (shards_of,), jnp.float32, low / len(split), high / len(split))
        return jnp.repeat(jnp.exp(steps), extent[axis_at] // shards_of).reshape((-1,) + (1,) * (len(extent) - axis_at - 1))

    loudness = one(*split[0])
    for cut in split[1:]:
        loudness = loudness * one(*cut)
    return loudness


def normal_values(rng, dims, width, most, split=(), held_as=jnp.bfloat16):
    entries = jax.random.normal(rng, dims, jnp.float32) * width
    if len(split) > 0:
        entries = level_of(rng, dims, split, -0.22, 0.18) * entries
    return jnp.clip(entries, min=-most, max=most).astype(held_as)


def setup_inputs(seed: int = 0) -> dict:
    arg_keys = jax.random.split(jax.random.key(seed), 6)
    return {
        "signal": normal_values(arg_keys[0], (CHANNELS, SEQ), 1.0, 6.0, ((0, 8), (1, 16))),
        "gate": normal_values(arg_keys[1], (CHANNELS, SEQ), 1.0, 6.0, ((0, 8), (1, 16))),
        "cotangent": normal_values(arg_keys[2], (CHANNELS, SEQ), 1.0, 6.0, ((0, 8), (1, 16))),
        "skip_gain": jnp.clip(0.5 + 1.0 * jax.random.uniform(arg_keys[3], (CHANNELS,), jnp.float32) ** level_of(arg_keys[3], (CHANNELS,), ((0, 8),), -0.2, 0.2), 0.5, 1.5),
        "filter_taps": normal_values(arg_keys[4], (CHAN_DEV, SEQ), SEQ ** -0.5, 0.01171875, ((1, 16),), jnp.float32),
    }


def cosine_sine(row_values, col_values, period):
    angle_value = (row_values[:, None] * col_values[None, :] % period).astype(jnp.float32) * (2.0 * math.pi / period)
    return (jnp.cos(angle_value), jnp.sin(angle_value))

def section_one(values, matrix, twist_cos, twist_sin):
    summed = jnp.einsum('cnj,nqk->cqkj', values.astype(jnp.float32), matrix.astype(jnp.float32))
    real_part = summed[:, 0] * twist_cos + summed[:, 1] * twist_sin
    imag_part = summed[:, 1] * twist_cos - summed[:, 0] * twist_sin
    return jnp.stack([real_part, imag_part], axis=1).astype(jnp.bfloat16)

def filter_section(values, matrix, twist_cos, twist_sin):
    summed = jnp.einsum('cnj,nqk->cqkj', values, matrix, precision=lax.Precision.HIGHEST)
    real_part = summed[:, 0] * twist_cos + summed[:, 1] * twist_sin
    imag_part = summed[:, 1] * twist_cos - summed[:, 0] * twist_sin
    return jnp.stack([real_part, imag_part], axis=1).astype(jnp.bfloat16)

def section_two(values, matrix):
    return jnp.einsum('cpkn,pnqm->cqkm', values.astype(jnp.float32), matrix.astype(jnp.float32))

def back_two(values, matrix, twist_cos, twist_sin):
    summed = jnp.einsum('cpkm,pmqn->cqkn', values.astype(jnp.float32), matrix.astype(jnp.float32))
    real_part = summed[:, 0] * twist_cos - summed[:, 1] * twist_sin
    imag_part = summed[:, 0] * twist_sin + summed[:, 1] * twist_cos
    return jnp.stack([real_part, imag_part], axis=1).astype(jnp.bfloat16)

def back_one(values, matrix):
    return jnp.einsum('cpkj,pkn->cnj', values.astype(jnp.float32), matrix.astype(jnp.float32))

def complex_product(former, latter):
    real_part = former[:, 0] * latter[:, 0] - former[:, 1] * latter[:, 1]
    imag_part = former[:, 0] * latter[:, 1] + former[:, 1] * latter[:, 0]
    return jnp.stack([real_part, imag_part], axis=1)

def conjugate_product(former, latter):
    real_part = former[:, 0] * latter[:, 0] + former[:, 1] * latter[:, 1]
    imag_part = former[:, 1] * latter[:, 0] - former[:, 0] * latter[:, 1]
    return jnp.stack([real_part, imag_part], axis=1)

def reference(signal, gate, cotangent, skip_gain, filter_taps):
    half_rows = N1 // 2
    points = N1 * N2
    n1_index = jnp.arange(half_rows, dtype=jnp.int32)
    k1_index = jnp.arange(N1, dtype=jnp.int32)
    n2_index = jnp.arange(N2, dtype=jnp.int32)
    cos_a, sin_a = cosine_sine(n1_index, k1_index, N1)
    matrix_one = jnp.stack([cos_a, -sin_a], axis=1).astype(jnp.bfloat16)
    filter_matrix = jnp.stack([cos_a, -sin_a], axis=1)
    cos_b, sin_b = cosine_sine(n2_index, n2_index, N2)
    matrix_two = jnp.stack([jnp.stack([cos_b, -sin_b], axis=1), jnp.stack([sin_b, cos_b], axis=1)], axis=0).astype(jnp.bfloat16)
    matrix_back_two = jnp.stack([jnp.stack([cos_b, sin_b], axis=1), jnp.stack([-sin_b, cos_b], axis=1)], axis=0).astype(jnp.bfloat16)
    cos_c, sin_c = cosine_sine(k1_index, n1_index, N1)
    matrix_back_one = (jnp.stack([cos_c, -sin_c], axis=0) / points).astype(jnp.bfloat16)
    twist_cos, twist_sin = cosine_sine(k1_index, n2_index, points)
    tap_grid = filter_taps.reshape(CHAN_DEV, half_rows, N2)
    filter_spec = section_two(filter_section(tap_grid, filter_matrix, twist_cos, twist_sin), matrix_two)

    def invert(spectrum):
        sectioned = back_two(spectrum.astype(jnp.bfloat16), matrix_back_two, twist_cos, twist_sin)
        return back_one(sectioned, matrix_back_one)

    def one_block(block_items):
        sig_rows, gate_rows, cot_rows, skip_rows = block_items
        sig_grid = sig_rows.reshape(CHAN_DEV, half_rows, N2)
        upstream = gate_rows.astype(jnp.float32) * cot_rows.astype(jnp.float32)
        up_grid = upstream.astype(jnp.bfloat16).reshape(CHAN_DEV, half_rows, N2)
        spec_signal = section_two(section_one(sig_grid, matrix_one, twist_cos, twist_sin), matrix_two)
        spec_up = section_two(section_one(up_grid, matrix_one, twist_cos, twist_sin), matrix_two)
        conv_half = invert(complex_product(spec_signal, filter_spec)).astype(jnp.bfloat16).reshape(CHAN_DEV, SEQ)
        corr_half = invert(conjugate_product(spec_up, filter_spec)).astype(jnp.bfloat16).reshape(CHAN_DEV, SEQ)
        taps_grad = invert(conjugate_product(spec_up, spec_signal))
        mixed_sum = conv_half.astype(jnp.float32) + skip_rows[:, None] * sig_rows.astype(jnp.float32)
        output = (gate_rows.astype(jnp.float32) * mixed_sum).astype(jnp.bfloat16)
        grad_gate = (cot_rows.astype(jnp.float32) * mixed_sum).astype(jnp.bfloat16)
        grad_signal = (corr_half.astype(jnp.float32) + skip_rows[:, None] * upstream).astype(jnp.bfloat16)
        return (output, grad_gate, grad_signal, taps_grad)
    results = lax.map(one_block, (signal.reshape(N_CH, CHAN_DEV, SEQ), gate.reshape(N_CH, CHAN_DEV, SEQ), cotangent.reshape(N_CH, CHAN_DEV, SEQ), skip_gain.reshape(N_CH, CHAN_DEV)))
    taps_total = lax.optimization_barrier(jnp.sum(results[3], axis=0)).reshape(CHAN_DEV, SEQ)
    grad_taps = taps_total / math.sqrt(SEQ)
    return (results[0].reshape(CHANNELS, SEQ), results[1].reshape(CHANNELS, SEQ), results[2].reshape(CHANNELS, SEQ), grad_taps)
```

```python
import math

import jax
import jax.numpy as jnp
import numpy as np
from jax import lax
from jax.sharding import PartitionSpec as P

N1 = 1024
N2 = 512
SEQ = 262144
HALF = N1 // 2
POINTS = N1 * N2


def tables():
    n1 = np.arange(HALF, dtype=np.int64)
    k1 = np.arange(HALF, dtype=np.int64)
    n2 = np.arange(N2, dtype=np.int64)
    ang_a = ((2 * k1 + 1)[:, None] * n1[None, :] % (2 * N1)) * (math.pi / N1)
    ang_b = (n2[:, None] * n2[None, :] % N2) * (2.0 * math.pi / N2)
    ang_t = ((2 * k1 + 1)[:, None] * n2[None, :] % (2 * POINTS)) * (math.pi / POINTS)
    first = np.concatenate([np.cos(ang_a), -np.sin(ang_a)], axis=0)
    cos_b, sin_b = np.cos(ang_b), np.sin(ang_b)
    second = np.block([[cos_b, -sin_b], [sin_b, cos_b]])
    back_second = np.block([[cos_b, sin_b], [-sin_b, cos_b]])
    back_first = 2.0 / POINTS * np.concatenate([np.cos(ang_a).T, -np.sin(ang_a).T], axis=1)
    half = lambda a: jnp.asarray(a.astype(np.float32)).astype(jnp.bfloat16)
    full = lambda a: jnp.asarray(a.astype(np.float32))
    return half(first), half(second), half(back_second), half(back_first), full(np.cos(ang_t)), full(np.sin(ang_t))


def body(signal, gate, cotangent, skip_gain, filter_taps):
    shards = lax.axis_size("ctx")
    channels = signal.shape[0]
    rows = signal.shape[1] // N2
    first, second, back_second, back_first, tw_cos, tw_sin = tables()

    def to_grid(values):
        blocks = values.reshape(channels, rows, N2)
        return lax.all_to_all(blocks, "ctx", split_axis=0, concat_axis=0, tiled=True).reshape(HALF, N2)

    def to_rows(grid):
        blocks = grid.astype(jnp.bfloat16).reshape(shards, rows, N2)
        return lax.all_to_all(blocks, "ctx", split_axis=0, concat_axis=0, tiled=True)

    def spectrum(grid):
        summed = jnp.dot(first, grid, preferred_element_type=jnp.float32)
        re, im = summed[:HALF], summed[HALF:]
        both = jnp.concatenate([re * tw_cos + im * tw_sin, im * tw_cos - re * tw_sin], axis=1)
        out = jnp.dot(both.astype(jnp.bfloat16), second, preferred_element_type=jnp.float32)
        return out[:, :N2], out[:, N2:]

    def invert(re, im):
        both = jnp.concatenate([re, im], axis=1).astype(jnp.bfloat16)
        out = jnp.dot(both, back_second, preferred_element_type=jnp.float32)
        re, im = out[:, :N2], out[:, N2:]
        stacked = jnp.concatenate([re * tw_cos - im * tw_sin, re * tw_sin + im * tw_cos], axis=0)
        return jnp.dot(back_first, stacked.astype(jnp.bfloat16), preferred_element_type=jnp.float32)

    def conj_product(a, b):
        return a[0] * b[0] + a[1] * b[1], a[1] * b[0] - a[0] * b[1]

    upstream = gate.astype(jnp.float32) * cotangent.astype(jnp.float32)
    spec_h = spectrum(to_grid(filter_taps.astype(jnp.bfloat16)))
    spec_x = spectrum(to_grid(signal))
    spec_u = spectrum(to_grid(upstream.astype(jnp.bfloat16)))
    product = spec_x[0] * spec_h[0] - spec_x[1] * spec_h[1], spec_x[0] * spec_h[1] + spec_x[1] * spec_h[0]
    conv = to_rows(invert(*product)).reshape(channels, rows * N2)
    taps = to_rows(invert(*conj_product(spec_u, spec_x)))
    corr = to_rows(invert(*conj_product(spec_u, spec_h))).reshape(channels, rows * N2)
    terms = lax.all_to_all(taps, "ch", split_axis=0, concat_axis=0, tiled=True)
    terms = terms.reshape(lax.axis_size("ch"), -1, rows, N2).astype(jnp.float32)
    grad_taps = (jnp.sum(terms, axis=0) / math.sqrt(SEQ)).reshape(-1, rows * N2)
    mixed = conv.astype(jnp.float32) + skip_gain[:, None] * signal.astype(jnp.float32)
    output = (gate.astype(jnp.float32) * mixed).astype(jnp.bfloat16)
    grad_gate = (cotangent.astype(jnp.float32) * mixed).astype(jnp.bfloat16)
    grad_signal = (corr.astype(jnp.float32) + skip_gain[:, None] * upstream).astype(jnp.bfloat16)
    return output, grad_gate, grad_signal, grad_taps


def solution(mesh):
    return jax.shard_map(
        body,
        mesh=mesh,
        in_specs=(P("ch", "ctx"), P("ch", "ctx"), P("ch", "ctx"), P("ch"), P(None, "ctx")),
        out_specs=(P("ch", "ctx"), P("ch", "ctx"), P("ch", "ctx"), P("ch", "ctx")),
        check_vma=False,
    )
```

```python
import functools
import math

import jax
import jax.numpy as jnp
import numpy as np
from jax import lax
from jax.experimental import pallas as pl
from jax.experimental.pallas import tpu as pltpu
from jax.sharding import PartitionSpec as P

N1 = 1024
N2 = 512
SEQ = 262144
HALF = N1 // 2
POINTS = N1 * N2
MESH = pl.DeviceIdType.MESH


def tables():
    n1 = np.arange(HALF, dtype=np.int64)
    k1 = np.arange(HALF, dtype=np.int64)
    n2 = np.arange(N2, dtype=np.int64)
    ang_a = ((2 * k1 + 1)[:, None] * n1[None, :] % (2 * N1)) * (math.pi / N1)
    ang_b = (n2[:, None] * n2[None, :] % N2) * (2.0 * math.pi / N2)
    ang_t = ((2 * k1 + 1)[:, None] * n2[None, :] % (2 * POINTS)) * (math.pi / POINTS)
    first = np.concatenate([np.cos(ang_a), -np.sin(ang_a)], axis=0)
    cos_b, sin_b = np.cos(ang_b), np.sin(ang_b)
    second = np.concatenate([cos_b, sin_b, cos_b, -sin_b, cos_b], axis=0)
    back_first = 2.0 / POINTS * np.concatenate([np.cos(ang_a).T, -np.sin(ang_a).T], axis=1)
    half = lambda a: jnp.asarray(a.astype(np.float32)).astype(jnp.bfloat16)
    full = lambda a: jnp.asarray(a.astype(np.float32))
    return half(first), half(second), half(back_first), full(np.cos(ang_t)), full(np.sin(ang_t))


def dot(a, b):
    return jnp.dot(a, b, preferred_element_type=jnp.float32)


def kernel(
    shards, chs, rows, block,
    sig_hbm, gate_hbm, cot_hbm, skip_ref, taps_hbm, first_hbm, second_hbm, back_hbm, twc_hbm, tws_hbm,
    out_ref, ggate_ref, gsig_ref, gtaps_ref,
    sig, gate, cot, taps, first, second, back, twc, tws,
    flat, send, recv, spec, both, stack, ysend, yrecv,
    load_sem, send_sem, recv_sem,
):
    me = lax.axis_index("ctx")
    ch = lax.axis_index("ch")
    own = shards // chs

    loads = [
        pltpu.make_async_copy(src, dst, load_sem.at[i])
        for i, (src, dst) in enumerate(
            [(sig_hbm, sig), (taps_hbm, taps), (gate_hbm, gate), (cot_hbm, cot), (first_hbm, first),
             (twc_hbm, twc), (tws_hbm, tws), (second_hbm, second), (back_hbm, back)]
        )
    ]
    for load in loads:
        load.start()

    barrier = pltpu.get_barrier_semaphore()

    def greet_ctx(step, carry):
        pl.semaphore_signal(barrier, inc=1, device_id={"ctx": lax.rem(me + step, shards)}, device_id_type=MESH)
        return carry

    lax.fori_loop(1, shards, greet_ctx, 0)

    def is_self(peer_ctx, peer_ch):
        return jnp.logical_and(peer_ctx == me, peer_ch == ch)

    def greet_owners(at, carry):
        peer_ctx, peer_ch = own * ch + lax.rem(at, own), at // own

        @pl.when(jnp.logical_not(is_self(peer_ctx, peer_ch)))
        def _():
            pl.semaphore_signal(
                barrier, inc=1, device_id={"ctx": peer_ctx, "ch": peer_ch}, device_id_type=MESH
            )

        return carry

    lax.fori_loop(0, shards, greet_owners, 0)

    def spread(which, value_at):
        def one(row, carry):
            for lane in range(N2 // 128):
                cols = pl.ds(pl.multiple_of(row * N2 + lane * 128, 128), 128)
                flat[lane, pl.ds(row, shards, stride=rows), :] = value_at(cols)
            return carry

        lax.fori_loop(0, rows, one, 0)

        def cast(at, carry):
            here = pl.ds(pl.multiple_of(at * rows, rows), rows)
            for lane in range(N2 // 128):
                send[which, at, :, lane * 128 : (lane + 1) * 128] = flat[lane, here, :].astype(jnp.bfloat16)
            return carry

        lax.fori_loop(0, shards, cast, 0)

    def remote(src, dst, which, slot_out, slot_in, device):
        return pltpu.make_async_remote_copy(
            src_ref=src, dst_ref=dst, send_sem=send_sem.at[which, slot_out], recv_sem=recv_sem.at[which, slot_in],
            device_id=device, device_id_type=MESH,
        )

    def exchange(which, src, dst):
        def one(step, carry):
            peer = lax.rem(me + step, shards)
            remote(src.at[peer], dst.at[me], which, peer, me, {"ctx": peer}).start()
            return carry

        pltpu.make_async_copy(src.at[me], dst.at[me], recv_sem.at[which, me]).start()
        lax.fori_loop(1, shards, one, 0)

    def arrive(which, src, dst):
        pltpu.make_async_copy(src.at[me], dst.at[me], recv_sem.at[which, me]).wait()

        def one(step, carry):
            peer = lax.rem(me + shards - step, shards)
            remote(src.at[peer], dst.at[peer], which, peer, peer, {"ctx": peer}).wait_recv()
            return carry

        lax.fori_loop(1, shards, one, 0)

    def drain(which, src, dst):
        def one(step, carry):
            peer = lax.rem(me + step, shards)
            remote(src.at[peer], dst.at[me], which, peer, me, {"ctx": peer}).wait_send()
            return carry

        lax.fori_loop(1, shards, one, 0)

    def twist(at):
        here = pl.ds(pl.multiple_of(at * block, block), block)
        return here, twc[here, :], tws[here, :]

    def forward(which):
        def one(at, carry):
            here, cos, sin = twist(at)
            grid = recv[which].reshape(HALF, N2)
            re = dot(first[here, :], grid)
            im = dot(first[pl.ds(pl.multiple_of(HALF + at * block, block), block), :], grid)
            both[:, :N2] = (re * cos + im * sin).astype(jnp.bfloat16)
            both[:, N2:] = (im * cos - re * sin).astype(jnp.bfloat16)
            spec[which, 0, here, :] = dot(both[...], second[: 2 * N2, :])
            spec[which, 1, here, :] = dot(both[...], second[3 * N2 :, :])
            return carry

        lax.fori_loop(0, HALF // block, one, 0)

    def inverse(slot, left, right, conj):
        def one(at, carry):
            here, cos, sin = twist(at)
            l_re, l_im = spec[left, 0, here, :], spec[left, 1, here, :]
            r_re, r_im = spec[right, 0, here, :], spec[right, 1, here, :]
            if conj:
                re, im = l_re * r_re + l_im * r_im, l_im * r_re - l_re * r_im
            else:
                re, im = l_re * r_re - l_im * r_im, l_re * r_im + l_im * r_re
            both[:, :N2] = re.astype(jnp.bfloat16)
            both[:, N2:] = im.astype(jnp.bfloat16)
            re = dot(both[...], second[2 * N2 : 4 * N2, :])
            im = dot(both[...], second[N2 : 3 * N2, :])
            stack[here, :] = (re * cos - im * sin).astype(jnp.bfloat16)
            stack[pl.ds(pl.multiple_of(HALF + at * block, block), block), :] = (re * sin + im * cos).astype(
                jnp.bfloat16
            )
            return carry

        lax.fori_loop(0, HALF // block, one, 0)

        def last(at, carry):
            here = pl.ds(pl.multiple_of(at * block, block), block)
            value = dot(back[here, :], stack[...]).astype(jnp.bfloat16)
            ysend[slot, pl.ds(at * (block // rows), block // rows)] = value.reshape(block // rows, rows, N2)
            return carry

        lax.fori_loop(0, HALF // block, last, 0)

    loads[0].wait()
    spread(0, lambda cols: sig[:, cols].astype(jnp.float32))
    pl.semaphore_wait(barrier, 2 * shards - 1 - jnp.where(me // own == ch, 1, 0))
    exchange(0, send.at[0], recv.at[0])
    loads[1].wait()
    spread(1, lambda cols: taps[:, cols])
    exchange(1, send.at[1], recv.at[1])
    loads[2].wait()
    loads[3].wait()
    spread(2, lambda cols: gate[:, cols].astype(jnp.float32) * cot[:, cols].astype(jnp.float32))
    exchange(2, send.at[2], recv.at[2])
    for load in loads[4:]:
        load.wait()
    arrive(0, send.at[0], recv.at[0])
    forward(0)
    arrive(1, send.at[1], recv.at[1])
    forward(1)
    inverse(0, 0, 1, False)
    exchange(3, ysend.at[0], yrecv.at[0])
    arrive(2, send.at[2], recv.at[2])
    forward(2)
    inverse(1, 2, 1, True)
    exchange(4, ysend.at[1], yrecv.at[1])
    inverse(2, 2, 0, True)

    mine = lax.rem(me, own) + own * ch
    owner = me // own

    def give(step, wait):
        peer = lax.rem(me + step, shards)
        local = is_self(peer, owner)

        @pl.when(local)
        def _():
            copy = pltpu.make_async_copy(ysend.at[2, peer], yrecv.at[2, mine], recv_sem.at[5, mine])
            copy.wait() if wait else copy.start()

        @pl.when(jnp.logical_not(local))
        def _():
            copy = remote(ysend.at[2, peer], yrecv.at[2, mine], 5, peer, mine, {"ctx": peer, "ch": owner})
            copy.wait_send() if wait else copy.start()

    def give_start(step, carry):
        give(step, False)
        return carry

    def give_wait(step, carry):
        give(step, True)
        return carry

    def take(at, carry):
        peer_ctx, peer_ch = own * ch + lax.rem(at, own), at // own

        @pl.when(jnp.logical_not(is_self(peer_ctx, peer_ch)))
        def _():
            remote(
                ysend.at[2, 0], yrecv.at[2, at], 5, 0, at, {"ctx": peer_ctx, "ch": peer_ch}
            ).wait_recv()

        return carry

    lax.fori_loop(0, shards, give_start, 0)

    def gather(slot):
        def one(at, carry):
            here = pl.ds(pl.multiple_of(at * rows, rows), rows)
            for lane in range(N2 // 128):
                flat[lane, here, :] = yrecv[slot, at, :, lane * 128 : (lane + 1) * 128].astype(jnp.float32)
            return carry

        lax.fori_loop(0, shards, one, 0)

    skip = skip_ref[...]
    arrive(3, ysend.at[0], yrecv.at[0])
    gather(0)

    def finish_conv(row, carry):
        for lane in range(N2 // 128):
            cols = pl.ds(pl.multiple_of(row * N2 + lane * 128, 128), 128)
            mixed = flat[lane, pl.ds(row, shards, stride=rows), :] + skip * sig[:, cols].astype(jnp.float32)
            out_ref[:, cols] = (gate[:, cols].astype(jnp.float32) * mixed).astype(jnp.bfloat16)
            ggate_ref[:, cols] = (cot[:, cols].astype(jnp.float32) * mixed).astype(jnp.bfloat16)
        return carry

    lax.fori_loop(0, rows, finish_conv, 0)
    arrive(4, ysend.at[1], yrecv.at[1])
    gather(1)

    def finish_corr(row, carry):
        for lane in range(N2 // 128):
            cols = pl.ds(pl.multiple_of(row * N2 + lane * 128, 128), 128)
            upstream = gate[:, cols].astype(jnp.float32) * cot[:, cols].astype(jnp.float32)
            corr = flat[lane, pl.ds(row, shards, stride=rows), :]
            gsig_ref[:, cols] = (corr + skip * upstream).astype(jnp.bfloat16)
        return carry

    lax.fori_loop(0, rows, finish_corr, 0)
    lax.fori_loop(0, shards, give_wait, 0)
    lax.fori_loop(0, shards, take, 0)
    scale = 1.0 / math.sqrt(SEQ)
    for group in range(own):
        total = yrecv[2, group].astype(jnp.float32)
        for at in range(1, chs):
            total = total + yrecv[2, own * at + group].astype(jnp.float32)
        for lane in range(N2 // 128):
            flat[lane, group * rows : (group + 1) * rows, :] = total[:, lane * 128 : (lane + 1) * 128] * scale

    def finish_taps(row, carry):
        for lane in range(N2 // 128):
            cols = pl.ds(pl.multiple_of(row * N2 + lane * 128, 128), 128)
            gtaps_ref[:, cols] = flat[lane, pl.ds(row, own, stride=rows), :]
        return carry

    lax.fori_loop(0, rows, finish_taps, 0)
    for which in range(3):
        drain(which, send.at[which], recv.at[which])
    drain(3, ysend.at[0], yrecv.at[0])
    drain(4, ysend.at[1], yrecv.at[1])


def body(shards, chs, signal, gate, cotangent, skip_gain, filter_taps):
    channels, positions = signal.shape
    rows = positions // N2
    own = shards // chs
    block = 256
    bf16, f32 = jnp.bfloat16, jnp.float32
    hbm = pl.BlockSpec(memory_space=pl.ANY)
    vmem = pl.BlockSpec(memory_space=pltpu.VMEM)
    return pl.pallas_call(
        functools.partial(kernel, shards, chs, rows, block),
        out_shape=[jax.ShapeDtypeStruct((channels, positions), bf16)] * 3
        + [jax.ShapeDtypeStruct((own, positions), f32)],
        in_specs=[hbm] * 3 + [vmem] + [hbm] * 6,
        out_specs=[vmem] * 4,
        scratch_shapes=[
            pltpu.VMEM((channels, positions), bf16),
            pltpu.VMEM((channels, positions), bf16),
            pltpu.VMEM((channels, positions), bf16),
            pltpu.VMEM((channels, positions), f32),
            pltpu.VMEM((2 * HALF, HALF), bf16),
            pltpu.VMEM((5 * N2, N2), bf16),
            pltpu.VMEM((HALF, 2 * HALF), bf16),
            pltpu.VMEM((HALF, N2), f32),
            pltpu.VMEM((HALF, N2), f32),
            pltpu.VMEM((N2 // 128, HALF, 128), f32),
            pltpu.VMEM((3, shards, rows, N2), bf16),
            pltpu.VMEM((3, shards, rows, N2), bf16),
            pltpu.VMEM((3, 2, HALF, N2), f32),
            pltpu.VMEM((block, 2 * N2), bf16),
            pltpu.VMEM((2 * HALF, N2), bf16),
            pltpu.VMEM((3, shards, rows, N2), bf16),
            pltpu.VMEM((3, shards, rows, N2), bf16),
            pltpu.SemaphoreType.DMA((9,)),
            pltpu.SemaphoreType.DMA((6, shards)),
            pltpu.SemaphoreType.DMA((6, shards)),
        ],
        compiler_params=pltpu.CompilerParams(
            collective_id=0, has_side_effects=True, vmem_limit_bytes=48 * 1024 * 1024
        ),
    )(signal, gate, cotangent, skip_gain.reshape(channels, 1), filter_taps, *tables())


def solution(mesh):
    return jax.shard_map(
        functools.partial(body, mesh.shape["ctx"], mesh.shape["ch"]),
        mesh=mesh,
        in_specs=(P("ch", "ctx"), P("ch", "ctx"), P("ch", "ctx"), P("ch"), P(None, "ctx")),
        out_specs=(P("ch", "ctx"), P("ch", "ctx"), P("ch", "ctx"), P("ch", "ctx")),
        check_vma=False,
    )
```

```python
import functools
import math

import jax
import jax.numpy as jnp
import numpy as np
from jax import lax
from jax.experimental import pallas as pl
from jax.experimental.pallas import tpu as pltpu
from jax.sharding import PartitionSpec as P

N1 = 1024
N2 = 512
SEQ = 262144
HALF = N1 // 2
POINTS = N1 * N2
MESH = pl.DeviceIdType.MESH


def tables():
    n1 = np.arange(HALF, dtype=np.int64)
    k1 = np.arange(HALF, dtype=np.int64)
    n2 = np.arange(N2, dtype=np.int64)
    ang_a = ((2 * k1 + 1)[:, None] * n1[None, :] % (2 * N1)) * (math.pi / N1)
    ang_b = (n2[:, None] * n2[None, :] % N2) * (2.0 * math.pi / N2)
    ang_t = ((2 * k1 + 1)[:, None] * n2[None, :] % (2 * POINTS)) * (math.pi / POINTS)
    first = np.concatenate([np.cos(ang_a), -np.sin(ang_a)], axis=0)
    cos_b, sin_b = np.cos(ang_b), np.sin(ang_b)
    second = np.concatenate([cos_b, sin_b, cos_b, -sin_b, cos_b], axis=0)
    back_first = 2.0 / POINTS * np.concatenate([np.cos(ang_a).T, -np.sin(ang_a).T], axis=1)
    half = lambda a: jnp.asarray(a.astype(np.float32)).astype(jnp.bfloat16)
    full = lambda a: jnp.asarray(a.astype(np.float32))
    return half(first), half(second), half(back_first), full(np.cos(ang_t)), full(np.sin(ang_t))


def dot(a, b):
    return jnp.dot(a, b, preferred_element_type=jnp.float32)


def kernel(
    shards, chs, rows, block,
    sig_hbm, gate_hbm, cot_hbm, gain_hbm, taps_hbm, first_hbm, second_hbm, back_hbm, twc_hbm, tws_hbm,
    out_ref, ggate_ref, gsig_ref, gtaps_ref,
    sig, gate, cot, gain, taps, first, second, back, twc, tws,
    flat, send, recv, hsend, hgrid, spec, both, stack, ysend, yrecv, tparts, tsend, trecv,
    load_sem, send_sem, recv_sem, share_send, share_recv,
):
    me = lax.axis_index("ctx")
    ch = lax.axis_index("ch")
    own = shards // chs
    tiles = N2 // 128
    quarter = shards // tiles
    hi, lo = ch // tiles, lax.rem(ch, tiles)

    loads = [
        pltpu.make_async_copy(src, dst, load_sem.at[i])
        for i, (src, dst) in enumerate(
            [(taps_hbm, taps), (sig_hbm, sig), (gate_hbm, gate), (cot_hbm, cot), (first_hbm, first),
             (twc_hbm, twc), (tws_hbm, tws), (second_hbm, second), (back_hbm, back), (gain_hbm, gain)]
        )
    ]
    for load in loads:
        load.start()

    barrier = pltpu.get_barrier_semaphore()

    def greet_ctx(step, carry):
        pl.semaphore_signal(barrier, inc=1, device_id={"ctx": lax.rem(me + step, shards)}, device_id_type=MESH)
        return carry

    lax.fori_loop(1, shards, greet_ctx, 0)

    def is_self(peer_ctx, peer_ch):
        return jnp.logical_and(peer_ctx == me, peer_ch == ch)

    def greet_line(step, carry):
        peer = hi * tiles + lax.rem(lo + step, tiles)
        pl.semaphore_signal(barrier, inc=1, device_id={"ch": peer}, device_id_type=MESH)
        return carry

    lax.fori_loop(1, tiles, greet_line, 0)
    alone = jnp.logical_and(me // own == ch, me // quarter == lo)

    def source(at):
        return own * ch + lax.rem(at, own), at // own * tiles + me // quarter

    def greet_sources(at, carry):
        peer_ctx, peer_ch = source(at)

        @pl.when(jnp.logical_not(is_self(peer_ctx, peer_ch)))
        def _():
            pl.semaphore_signal(
                barrier, inc=1, device_id={"ctx": peer_ctx, "ch": peer_ch}, device_id_type=MESH
            )

        return carry

    lax.fori_loop(0, quarter, greet_sources, 0)

    def spread(which, value_at):
        def one(row, carry):
            for lane in range(N2 // 128):
                cols = pl.ds(pl.multiple_of(row * N2 + lane * 128, 128), 128)
                flat[lane, pl.ds(row, shards, stride=rows), :] = value_at(cols)
            return carry

        lax.fori_loop(0, rows, one, 0, unroll=8)

        def cast(at, carry):
            here = pl.ds(pl.multiple_of(at * rows, rows), rows)
            for lane in range(N2 // 128):
                send[which, at, :, lane * 128 : (lane + 1) * 128] = flat[lane, here, :].astype(jnp.bfloat16)
            return carry

        lax.fori_loop(0, shards, cast, 0, unroll=4)

    def remote(src, dst, which, slot_out, slot_in, device):
        return pltpu.make_async_remote_copy(
            src_ref=src, dst_ref=dst, send_sem=send_sem.at[which, slot_out], recv_sem=recv_sem.at[which, slot_in],
            device_id=device, device_id_type=MESH,
        )

    def exchange(which, src, dst):
        def one(step, carry):
            peer = lax.rem(me + step, shards)
            remote(src.at[peer], dst.at[me], which, peer, me, {"ctx": peer}).start()
            return carry

        pltpu.make_async_copy(src.at[me], dst.at[me], recv_sem.at[which, me]).start()
        lax.fori_loop(1, shards, one, 0)

    def arrive(which, src, dst):
        pltpu.make_async_copy(src.at[me], dst.at[me], recv_sem.at[which, me]).wait()

        def one(step, carry):
            peer = lax.rem(me + shards - step, shards)
            remote(src.at[peer], dst.at[peer], which, peer, peer, {"ctx": peer}).wait_recv()
            return carry

        lax.fori_loop(1, shards, one, 0)

    def drain(which, src, dst):
        def one(step, carry):
            peer = lax.rem(me + step, shards)
            remote(src.at[peer], dst.at[me], which, peer, me, {"ctx": peer}).wait_send()
            return carry

        lax.fori_loop(1, shards, one, 0)

    def twist(at):
        here = pl.ds(pl.multiple_of(at * block, block), block)
        return here, twc[here, :], tws[here, :]

    def forward(which, load_grid):
        def one(at, carry):
            here, cos, sin = twist(at)
            grid = load_grid()
            re = dot(first[here, :], grid)
            im = dot(first[pl.ds(pl.multiple_of(HALF + at * block, block), block), :], grid)
            both[:, :N2] = (re * cos + im * sin).astype(jnp.bfloat16)
            both[:, N2:] = (im * cos - re * sin).astype(jnp.bfloat16)
            spec[which, 0, here, :] = dot(both[...], second[: 2 * N2, :])
            spec[which, 1, here, :] = dot(both[...], second[3 * N2 :, :])
            return carry

        lax.fori_loop(0, HALF // block, one, 0)

    def inverse(slot, left, right, conj):
        def one(at, carry):
            here, cos, sin = twist(at)
            l_re, l_im = spec[left, 0, here, :], spec[left, 1, here, :]
            r_re, r_im = spec[right, 0, here, :], spec[right, 1, here, :]
            if conj:
                re, im = l_re * r_re + l_im * r_im, l_im * r_re - l_re * r_im
            else:
                re, im = l_re * r_re - l_im * r_im, l_re * r_im + l_im * r_re
            both[:, :N2] = re.astype(jnp.bfloat16)
            both[:, N2:] = im.astype(jnp.bfloat16)
            re = dot(both[...], second[2 * N2 : 4 * N2, :])
            im = dot(both[...], second[N2 : 3 * N2, :])
            stack[here, :] = (re * cos - im * sin).astype(jnp.bfloat16)
            stack[pl.ds(pl.multiple_of(HALF + at * block, block), block), :] = (re * sin + im * cos).astype(
                jnp.bfloat16
            )
            return carry

        lax.fori_loop(0, HALF // block, one, 0)

        def last(at, carry):
            here = pl.ds(pl.multiple_of(at * block, block), block)
            value = dot(back[here, :], stack[...]).astype(jnp.bfloat16)
            ysend[slot, pl.ds(at * (block // rows), block // rows)] = value.reshape(block // rows, rows, N2)
            return carry

        lax.fori_loop(0, HALF // block, last, 0)

    def share(step):
        return lax.rem(lo + step, tiles)

    def taps_columns(step):
        return pltpu.make_async_remote_copy(
            src_ref=hgrid.at[lo], dst_ref=hgrid.at[lo], send_sem=share_send.at[0, step],
            recv_sem=share_recv.at[0, step], device_id={"ch": hi * tiles + share(step)}, device_id_type=MESH,
        )

    def tap_terms(step):
        return pltpu.make_async_remote_copy(
            src_ref=ysend.at[2, pl.ds(share(step) * quarter, quarter)], dst_ref=tparts.at[step],
            send_sem=share_send.at[1, step], recv_sem=share_recv.at[1, step],
            device_id={"ch": hi * tiles + share(step)}, device_id_type=MESH,
        )

    loads[0].wait()

    def column(row, carry):
        cols = pl.ds(pl.multiple_of(row * N2 + lo * 128, 128), 128)
        flat[0, pl.ds(row, shards, stride=rows), :] = taps[:, cols]
        return carry

    lax.fori_loop(0, rows, column, 0, unroll=8)

    def cast_column(at, carry):
        hsend[at] = flat[0, pl.ds(pl.multiple_of(at * rows, rows), rows), :].astype(jnp.bfloat16)
        return carry

    lax.fori_loop(0, shards, cast_column, 0, unroll=4)
    pl.semaphore_wait(barrier, shards - 1 + tiles - 1 + quarter - jnp.where(alone, 1, 0))
    exchange(1, hsend, hgrid.at[lo])
    loads[1].wait()
    spread(0, lambda cols: sig[:, cols].astype(jnp.float32))
    exchange(0, send.at[0], recv.at[0])
    loads[2].wait()
    loads[3].wait()
    spread(1, lambda cols: gate[:, cols].astype(jnp.float32) * cot[:, cols].astype(jnp.float32))
    exchange(2, send.at[1], recv.at[1])
    for load in loads[4:]:
        load.wait()
    arrive(1, hsend, hgrid.at[lo])
    for step in range(1, tiles):
        taps_columns(step).start()
    arrive(0, send.at[0], recv.at[0])
    forward(0, lambda: recv[0].reshape(HALF, N2))
    for step in range(1, tiles):
        taps_columns(step).wait_recv()
    forward(1, lambda: jnp.concatenate([hgrid[tile].reshape(HALF, 128) for tile in range(tiles)], axis=1))
    inverse(0, 0, 1, False)
    exchange(3, ysend.at[0], yrecv.at[0])
    arrive(2, send.at[1], recv.at[1])
    forward(2, lambda: recv[1].reshape(HALF, N2))
    inverse(2, 2, 0, True)
    for step in range(1, tiles):
        tap_terms(step).start()
    inverse(1, 2, 1, True)
    exchange(4, ysend.at[1], yrecv.at[1])

    for step in range(1, tiles):
        tap_terms(step).wait_recv()
    for at in range(quarter):
        total = ysend[2, lo * quarter + at].astype(jnp.float32)
        for step in range(1, tiles):
            total = total + tparts[step, at].astype(jnp.float32)
        tsend[at] = total.astype(jnp.bfloat16)

    slot = hi * own + lax.rem(me, own)
    owner = me // own

    def give(at, wait):
        peer = lo * quarter + at
        local = is_self(peer, owner)

        @pl.when(local)
        def _():
            copy = pltpu.make_async_copy(tsend.at[at], trecv.at[slot], recv_sem.at[5, slot])
            copy.wait() if wait else copy.start()

        @pl.when(jnp.logical_not(local))
        def _():
            copy = remote(tsend.at[at], trecv.at[slot], 5, at, slot, {"ctx": peer, "ch": owner})
            copy.wait_send() if wait else copy.start()

    for at in range(quarter):
        give(at, False)

    def take(at):
        peer_ctx, peer_ch = source(at)

        @pl.when(jnp.logical_not(is_self(peer_ctx, peer_ch)))
        def _():
            remote(tsend.at[0], trecv.at[at], 5, 0, at, {"ctx": peer_ctx, "ch": peer_ch}).wait_recv()

    def gather(slot):
        def one(at, carry):
            here = pl.ds(pl.multiple_of(at * rows, rows), rows)
            for lane in range(N2 // 128):
                flat[lane, here, :] = yrecv[slot, at, :, lane * 128 : (lane + 1) * 128].astype(jnp.float32)
            return carry

        lax.fori_loop(0, shards, one, 0, unroll=4)

    channel = lax.broadcasted_iota(jnp.int32, (shards, 128), 0)
    skip = jnp.zeros((shards, 128), jnp.float32)
    for at in range(shards):
        skip = jnp.where(channel == at, gain[at], skip)
    arrive(3, ysend.at[0], yrecv.at[0])
    gather(0)

    def finish_conv(row, carry):
        for lane in range(N2 // 128):
            cols = pl.ds(pl.multiple_of(row * N2 + lane * 128, 128), 128)
            mixed = flat[lane, pl.ds(row, shards, stride=rows), :] + skip * sig[:, cols].astype(jnp.float32)
            out_ref[:, cols] = (gate[:, cols].astype(jnp.float32) * mixed).astype(jnp.bfloat16)
            ggate_ref[:, cols] = (cot[:, cols].astype(jnp.float32) * mixed).astype(jnp.bfloat16)
        return carry

    lax.fori_loop(0, rows, finish_conv, 0, unroll=8)
    arrive(4, ysend.at[1], yrecv.at[1])
    gather(1)

    def finish_corr(row, carry):
        for lane in range(N2 // 128):
            cols = pl.ds(pl.multiple_of(row * N2 + lane * 128, 128), 128)
            upstream = gate[:, cols].astype(jnp.float32) * cot[:, cols].astype(jnp.float32)
            corr = flat[lane, pl.ds(row, shards, stride=rows), :]
            gsig_ref[:, cols] = (corr + skip * upstream).astype(jnp.bfloat16)
        return carry

    lax.fori_loop(0, rows, finish_corr, 0, unroll=8)
    for at in range(quarter):
        give(at, True)
    for at in range(quarter):
        take(at)
    scale = 1.0 / math.sqrt(SEQ)
    for group in range(own):
        total = trecv[group].astype(jnp.float32)
        for at in range(own + group, quarter, own):
            total = total + trecv[at].astype(jnp.float32)
        for lane in range(N2 // 128):
            flat[lane, group * rows : (group + 1) * rows, :] = total[:, lane * 128 : (lane + 1) * 128] * scale

    def finish_taps(row, carry):
        for lane in range(N2 // 128):
            cols = pl.ds(pl.multiple_of(row * N2 + lane * 128, 128), 128)
            gtaps_ref[:, cols] = flat[lane, pl.ds(row, own, stride=rows), :]
        return carry

    lax.fori_loop(0, rows, finish_taps, 0, unroll=8)
    drain(1, hsend, hgrid.at[lo])
    drain(0, send.at[0], recv.at[0])
    drain(2, send.at[1], recv.at[1])
    for step in range(1, tiles):
        taps_columns(step).wait_send()
        tap_terms(step).wait_send()
    drain(3, ysend.at[0], yrecv.at[0])
    drain(4, ysend.at[1], yrecv.at[1])


def emit(*refs):
    copies = [pltpu.make_async_copy(refs[at], refs[4 + at], refs[8].at[at]) for at in range(4)]
    for copy in copies:
        copy.start()
    for copy in copies:
        copy.wait()


def body(shards, chs, signal, gate, cotangent, skip_gain, filter_taps):
    channels, positions = signal.shape
    rows = positions // N2
    own = shards // chs
    block = 256
    bf16, f32 = jnp.bfloat16, jnp.float32
    hbm = pl.BlockSpec(memory_space=pl.ANY)
    vmem = pl.BlockSpec(memory_space=pltpu.VMEM)
    operands = signal, gate, cotangent, skip_gain, filter_taps, *tables()
    results = pl.pallas_call(
        functools.partial(kernel, shards, chs, rows, block),
        out_shape=[jax.ShapeDtypeStruct((channels, positions), bf16)] * 3
        + [jax.ShapeDtypeStruct((own, positions), f32)],
        in_specs=[hbm] * 10,
        out_specs=[vmem] * 4,
        scratch_shapes=[
            pltpu.VMEM((channels, positions), bf16),
            pltpu.VMEM((channels, positions), bf16),
            pltpu.VMEM((channels, positions), bf16),
            pltpu.SMEM((channels,), f32),
            pltpu.VMEM((channels, positions), f32),
            pltpu.VMEM((2 * HALF, HALF), bf16),
            pltpu.VMEM((5 * N2, N2), bf16),
            pltpu.VMEM((HALF, 2 * HALF), bf16),
            pltpu.VMEM((HALF, N2), f32),
            pltpu.VMEM((HALF, N2), f32),
            pltpu.VMEM((N2 // 128, HALF, 128), f32),
            pltpu.VMEM((2, shards, rows, N2), bf16),
            pltpu.VMEM((2, shards, rows, N2), bf16),
            pltpu.VMEM((shards, rows, 128), bf16),
            pltpu.VMEM((N2 // 128, shards, rows, 128), bf16),
            pltpu.VMEM((3, 2, HALF, N2), f32),
            pltpu.VMEM((block, 2 * N2), bf16),
            pltpu.VMEM((2 * HALF, N2), bf16),
            pltpu.VMEM((3, shards, rows, N2), bf16),
            pltpu.VMEM((2, shards, rows, N2), bf16),
            pltpu.VMEM((N2 // 128, shards * 128 // N2, rows, N2), bf16),
            pltpu.VMEM((shards * 128 // N2, rows, N2), bf16),
            pltpu.VMEM((shards * 128 // N2, rows, N2), bf16),
            pltpu.SemaphoreType.DMA((10,)),
            pltpu.SemaphoreType.DMA((6, shards)),
            pltpu.SemaphoreType.DMA((6, shards)),
            pltpu.SemaphoreType.DMA((2, N2 // 128)),
            pltpu.SemaphoreType.DMA((2, N2 // 128)),
        ],
        compiler_params=pltpu.CompilerParams(
            collective_id=0, has_side_effects=True, vmem_limit_bytes=48 * 1024 * 1024
        ),
    )(*[pltpu.with_memory_space_constraint(operand, pltpu.HBM) for operand in operands])
    return pl.pallas_call(
        emit,
        out_shape=[jax.ShapeDtypeStruct(result.shape, result.dtype) for result in results],
        in_specs=[hbm] * 4,
        out_specs=[hbm] * 4,
        scratch_shapes=[pltpu.SemaphoreType.DMA((4,))],
        compiler_params=pltpu.CompilerParams(vmem_limit_bytes=1024 * 1024),
    )(*results)


def solution(mesh):
    return jax.shard_map(
        functools.partial(body, mesh.shape["ctx"], mesh.shape["ch"]),
        mesh=mesh,
        in_specs=(P("ch", "ctx"), P("ch", "ctx"), P("ch", "ctx"), P("ch"), P(None, "ctx")),
        out_specs=(P("ch", "ctx"), P("ch", "ctx"), P("ch", "ctx"), P("ch", "ctx")),
        check_vma=False,
    )
```

```python
import functools
import math

import jax
import jax.numpy as jnp
import numpy as np
from jax import lax
from jax.experimental import pallas as pl
from jax.experimental.pallas import tpu as pltpu
from jax.sharding import PartitionSpec as P

N1 = 1024
N2 = 512
SEQ = 262144
HALF = N1 // 2
POINTS = N1 * N2
MESH = pl.DeviceIdType.MESH


def tables():
    quart, pair = HALF // 2, N2 // 2
    k1 = np.arange(quart, dtype=np.int64)
    n1 = np.arange(HALF, dtype=np.int64)
    n2 = np.arange(N2, dtype=np.int64)
    rows = np.concatenate([k1, HALF - 1 - k1])
    ang_a = ((2 * k1 + 1)[:, None] * n1[None, :] % (2 * N1)) * (math.pi / N1)
    ang_b = (n2[:, None] * n2[None, : pair + 1] % N2) * (2.0 * math.pi / N2)
    ang_t = ((2 * rows + 1)[:, None] * n2[None, :] % (2 * POINTS)) * (math.pi / POINTS)
    first = np.concatenate([np.cos(ang_a), -np.sin(ang_a)], axis=0)
    first = np.stack([first[:, 0::2], first[:, 1::2]])
    cos_b, sin_b = np.cos(ang_b), np.sin(ang_b)
    second = np.concatenate([cos_b[:, :pair], cos_b[:, pair:], sin_b[:, 1:pair]], axis=1)
    half = lambda a: jnp.asarray(np.ascontiguousarray(a).astype(np.float32)).astype(jnp.bfloat16)
    full = lambda a: jnp.asarray(a.astype(np.float32))
    return (
        half(first), half(second), half(second.T), half(2.0 / POINTS * first.transpose(0, 2, 1)),
        full(np.cos(ang_t)), full(np.sin(ang_t)),
    )


def dot(a, b):
    return jnp.dot(a, b, preferred_element_type=jnp.float32)


def kernel(
    shards, chs, rows, block,
    sig_hbm, gate_hbm, cot_hbm, gain_hbm, taps_hbm, first_hbm, second_hbm, under_hbm, back_hbm, twc_hbm, tws_hbm,
    out_ref, ggate_ref, gsig_ref, gtaps_ref,
    sig, gate, cot, gain, taps, first, second, under, back, twc, tws,
    flat, send, recv, hsend, hgrid, spec, both, stack, ysend, yrecv, tparts, tsend, trecv,
    load_sem, send_sem, recv_sem, share_send, share_recv,
):
    me = lax.axis_index("ctx")
    ch = lax.axis_index("ch")
    own = shards // chs
    tiles = N2 // 128
    quarter = shards // tiles
    hi, lo = ch // tiles, lax.rem(ch, tiles)

    loads = [
        pltpu.make_async_copy(src, dst, load_sem.at[i])
        for i, (src, dst) in enumerate(
            [(taps_hbm, taps), (sig_hbm, sig), (gate_hbm, gate), (cot_hbm, cot), (first_hbm, first),
             (twc_hbm, twc), (tws_hbm, tws), (second_hbm, second), (under_hbm, under), (back_hbm, back), (gain_hbm, gain)]
        )
    ]
    for load in loads:
        load.start()

    barrier = pltpu.get_barrier_semaphore()

    def greet_ctx(step, carry):
        pl.semaphore_signal(barrier, inc=1, device_id={"ctx": lax.rem(me + step, shards)}, device_id_type=MESH)
        return carry

    lax.fori_loop(1, shards, greet_ctx, 0)

    def is_self(peer_ctx, peer_ch):
        return jnp.logical_and(peer_ctx == me, peer_ch == ch)

    def greet_line(step, carry):
        peer = hi * tiles + lax.rem(lo + step, tiles)
        pl.semaphore_signal(barrier, inc=1, device_id={"ch": peer}, device_id_type=MESH)
        return carry

    lax.fori_loop(1, tiles, greet_line, 0)
    alone = jnp.logical_and(me // own == ch, me // quarter == lo)

    def source(at):
        return own * ch + lax.rem(at, own), at // own * tiles + me // quarter

    def greet_sources(at, carry):
        peer_ctx, peer_ch = source(at)

        @pl.when(jnp.logical_not(is_self(peer_ctx, peer_ch)))
        def _():
            pl.semaphore_signal(
                barrier, inc=1, device_id={"ctx": peer_ctx, "ch": peer_ch}, device_id_type=MESH
            )

        return carry

    lax.fori_loop(0, quarter, greet_sources, 0)

    def place(row):
        return row // 2 + lax.rem(row, 2) * (rows // 2)

    def spread(which, value_at):
        def one(row, carry):
            for lane in range(N2 // 128):
                cols = pl.ds(pl.multiple_of(row * N2 + lane * 128, 128), 128)
                flat[lane, pl.ds(place(row), shards, stride=rows), :] = value_at(cols)
            return carry

        lax.fori_loop(0, rows, one, 0, unroll=8)

        def cast(at, carry):
            here = pl.ds(pl.multiple_of(at * rows, rows), rows)
            for lane in range(N2 // 128):
                send[which, at, :, lane * 128 : (lane + 1) * 128] = flat[lane, here, :].astype(jnp.bfloat16)
            return carry

        lax.fori_loop(0, shards, cast, 0, unroll=4)

    def remote(src, dst, which, slot_out, slot_in, device):
        return pltpu.make_async_remote_copy(
            src_ref=src, dst_ref=dst, send_sem=send_sem.at[which, slot_out], recv_sem=recv_sem.at[which, slot_in],
            device_id=device, device_id_type=MESH,
        )

    def peer_of(step):
        return lax.rem(me + step, shards)

    def outgoing(which, src, dst, peer):
        return remote(src.at[peer], dst.at[me], which, peer, me, {"ctx": peer})

    def each(first, last, action):
        def one(step, carry):
            action(step)
            return carry

        lax.fori_loop(first, last, one, 0, unroll=True)

    def keep(which, src, dst):
        return pltpu.make_async_copy(src.at[me], dst.at[me], recv_sem.at[which, me])

    def exchange(which, src, dst):
        each(1, shards, lambda step: outgoing(which, src, dst, peer_of(step)).start())
        keep(which, src, dst).start()

    def arrive(which, src, dst):
        keep(which, src, dst).wait()

        def take_one(step):
            peer = peer_of(step)
            remote(src.at[peer], dst.at[peer], which, peer, peer, {"ctx": peer}).wait_recv()

        each(1, shards, take_one)

    def drain(which, src, dst):
        each(1, shards, lambda step: outgoing(which, src, dst, peer_of(step)).wait_send())

    quart, pair = HALF // 2, N2 // 2
    edge = lax.broadcasted_iota(jnp.int32, (block, pair), 1) == 0

    def forward(which, load_grid):
        for at in range(quart // block):
            here = slice(at * block, (at + 1) * block)
            there = slice(quart + at * block, quart + (at + 1) * block)
            even, odd = load_grid()
            e_re, o_re = dot(first[0, here, :], even), dot(first[1, here, :], odd)
            e_im, o_im = dot(first[0, there, :], even), dot(first[1, there, :], odd)
            for part, rows_at, re, im in (
                (0, here, e_re + o_re, e_im + o_im), (1, there, e_re - o_re, o_im - e_im)
            ):
                cos, sin = twc[rows_at, :], tws[rows_at, :]
                both[at, part] = (re * cos + im * sin).astype(jnp.bfloat16)
                both[at, 2 + part] = (im * cos - re * sin).astype(jnp.bfloat16)
            summed = dot(both[at].reshape(4 * block, N2), second[...]).reshape(4, block, N2)
            for part, rows_at in ((0, here), (1, there)):
                r_c, r_s = summed[part][:, :pair], summed[part][:, pair:]
                i_c, i_s = summed[2 + part][:, :pair], summed[2 + part][:, pair:]
                spec[which, 0, rows_at, :pair] = jnp.where(edge, r_c, r_c + i_s)
                spec[which, 0, rows_at, pair:] = jnp.where(edge, r_s, r_c - i_s)
                spec[which, 1, rows_at, :pair] = jnp.where(edge, i_c, i_c - r_s)
                spec[which, 1, rows_at, pair:] = jnp.where(edge, i_s, i_c + r_s)

    def product(left, right, conj, rows_at, cols):
        l_re, l_im = spec[left, 0, rows_at, cols], spec[left, 1, rows_at, cols]
        r_re, r_im = spec[right, 0, rows_at, cols], spec[right, 1, rows_at, cols]
        if conj:
            return l_re * r_re + l_im * r_im, l_im * r_re - l_re * r_im
        return l_re * r_re - l_im * r_im, l_re * r_im + l_im * r_re

    def inverse(slot, left, right, conj):
        for at in range(quart // block):
            here = slice(at * block, (at + 1) * block)
            there = slice(quart + at * block, quart + (at + 1) * block)
            for part, rows_at in ((0, here), (1, there)):
                lo_re, lo_im = product(left, right, conj, rows_at, slice(0, pair))
                hi_re, hi_im = product(left, right, conj, rows_at, slice(pair, N2))
                both[at, part, :, :pair] = jnp.where(edge, lo_re, lo_re + hi_re).astype(jnp.bfloat16)
                both[at, part, :, pair:] = jnp.where(edge, hi_re, hi_im - lo_im).astype(jnp.bfloat16)
                both[at, 2 + part, :, :pair] = jnp.where(edge, lo_im, lo_im + hi_im).astype(jnp.bfloat16)
                both[at, 2 + part, :, pair:] = jnp.where(edge, hi_im, lo_re - hi_re).astype(jnp.bfloat16)
            summed = dot(both[at].reshape(4 * block, N2), under[...]).reshape(4, block, N2)
            twisted = []
            for part, rows_at in ((0, here), (1, there)):
                cos, sin = twc[rows_at, :], tws[rows_at, :]
                re, im = summed[part], summed[2 + part]
                twisted.append((re * cos - im * sin, re * sin + im * cos))
            (lo_re, lo_im), (hi_re, hi_im) = twisted
            stack[0, here, :] = (lo_re + hi_re).astype(jnp.bfloat16)
            stack[0, there, :] = (lo_im - hi_im).astype(jnp.bfloat16)
            stack[1, here, :] = (lo_re - hi_re).astype(jnp.bfloat16)
            stack[1, there, :] = (lo_im + hi_im).astype(jnp.bfloat16)
        for odd in range(2):
            value = dot(back[odd], stack[odd]).astype(jnp.bfloat16)
            ysend[slot, :, odd * (rows // 2) : (odd + 1) * (rows // 2)] = value.reshape(shards, rows // 2, N2)

    def share(step):
        return lax.rem(lo + step, tiles)

    def taps_columns(step):
        return pltpu.make_async_remote_copy(
            src_ref=hgrid.at[lo], dst_ref=hgrid.at[lo], send_sem=share_send.at[0, step],
            recv_sem=share_recv.at[0, step], device_id={"ch": hi * tiles + share(step)}, device_id_type=MESH,
        )

    def tap_terms(step):
        return pltpu.make_async_remote_copy(
            src_ref=ysend.at[2, pl.ds(share(step) * quarter, quarter)], dst_ref=tparts.at[step],
            send_sem=share_send.at[1, step], recv_sem=share_recv.at[1, step],
            device_id={"ch": hi * tiles + share(step)}, device_id_type=MESH,
        )

    loads[0].wait()

    def column(row, carry):
        cols = pl.ds(pl.multiple_of(row * N2 + lo * 128, 128), 128)
        flat[0, pl.ds(place(row), shards, stride=rows), :] = taps[:, cols]
        return carry

    lax.fori_loop(0, rows, column, 0, unroll=8)

    def cast_column(at, carry):
        hsend[at] = flat[0, pl.ds(pl.multiple_of(at * rows, rows), rows), :].astype(jnp.bfloat16)
        return carry

    lax.fori_loop(0, shards, cast_column, 0, unroll=4)
    loads[1].wait()
    spread(0, lambda cols: sig[:, cols].astype(jnp.float32))
    loads[2].wait()
    loads[3].wait()
    for load in loads[4:]:
        load.wait()
    pl.semaphore_wait(barrier, shards - 1 + tiles - 1 + quarter - jnp.where(alone, 1, 0))
    exchange(1, hsend, hgrid.at[lo])
    exchange(0, send.at[0], recv.at[0])
    arrive(1, hsend, hgrid.at[lo])
    for step in range(1, tiles):
        taps_columns(step).start()

    spread(1, lambda cols: gate[:, cols].astype(jnp.float32) * cot[:, cols].astype(jnp.float32))
    exchange(2, send.at[1], recv.at[1])
    arrive(0, send.at[0], recv.at[0])

    def arrived(which):
        return [
            recv[which, :, odd * (rows // 2) : (odd + 1) * (rows // 2), :].reshape(HALF // 2, N2) for odd in range(2)
        ]

    def arrived_taps():
        tile = lambda at, odd: hgrid[at, :, odd * (rows // 2) : (odd + 1) * (rows // 2), :].reshape(HALF // 2, 128)
        return [jnp.concatenate([tile(at, odd) for at in range(tiles)], axis=1) for odd in range(2)]

    forward(0, lambda: arrived(0))
    for step in range(1, tiles):
        taps_columns(step).wait_recv()
    forward(1, arrived_taps)
    inverse(0, 0, 1, False)
    exchange(3, ysend.at[0], yrecv.at[0])
    arrive(2, send.at[1], recv.at[1])
    forward(2, lambda: arrived(1))
    inverse(2, 2, 0, True)
    for step in range(1, tiles):
        tap_terms(step).start()
    inverse(1, 2, 1, True)
    exchange(4, ysend.at[1], yrecv.at[1])

    for step in range(1, tiles):
        tap_terms(step).wait_recv()
    for at in range(quarter):
        total = ysend[2, lo * quarter + at].astype(jnp.float32)
        for step in range(1, tiles):
            total = total + tparts[step, at].astype(jnp.float32)
        tsend[at] = total.astype(jnp.bfloat16)

    slot = hi * own + lax.rem(me, own)
    owner = me // own

    def give(at, wait):
        peer = lo * quarter + at
        local = is_self(peer, owner)

        @pl.when(local)
        def _():
            copy = pltpu.make_async_copy(tsend.at[at], trecv.at[slot], recv_sem.at[5, slot])
            copy.wait() if wait else copy.start()

        @pl.when(jnp.logical_not(local))
        def _():
            copy = remote(tsend.at[at], trecv.at[slot], 5, at, slot, {"ctx": peer, "ch": owner})
            copy.wait_send() if wait else copy.start()

    for at in range(quarter):
        give(at, False)

    def take(at):
        peer_ctx, peer_ch = source(at)

        @pl.when(jnp.logical_not(is_self(peer_ctx, peer_ch)))
        def _():
            remote(tsend.at[0], trecv.at[at], 5, 0, at, {"ctx": peer_ctx, "ch": peer_ch}).wait_recv()

    def gather(slot):
        def one(at, carry):
            here = pl.ds(pl.multiple_of(at * rows, rows), rows)
            for lane in range(N2 // 128):
                flat[lane, here, :] = yrecv[slot, at, :, lane * 128 : (lane + 1) * 128].astype(jnp.float32)
            return carry

        lax.fori_loop(0, shards, one, 0, unroll=4)

    channel = lax.broadcasted_iota(jnp.int32, (shards, 128), 0)
    skip = jnp.zeros((shards, 128), jnp.float32)
    for at in range(shards):
        skip = jnp.where(channel == at, gain[at], skip)
    arrive(3, ysend.at[0], yrecv.at[0])
    gather(0)

    def finish_conv(row, carry):
        for lane in range(N2 // 128):
            cols = pl.ds(pl.multiple_of(row * N2 + lane * 128, 128), 128)
            mixed = flat[lane, pl.ds(place(row), shards, stride=rows), :] + skip * sig[:, cols].astype(jnp.float32)
            out_ref[:, cols] = (gate[:, cols].astype(jnp.float32) * mixed).astype(jnp.bfloat16)
            ggate_ref[:, cols] = (cot[:, cols].astype(jnp.float32) * mixed).astype(jnp.bfloat16)
        return carry

    lax.fori_loop(0, rows, finish_conv, 0, unroll=8)
    arrive(4, ysend.at[1], yrecv.at[1])
    gather(1)

    def finish_corr(row, carry):
        for lane in range(N2 // 128):
            cols = pl.ds(pl.multiple_of(row * N2 + lane * 128, 128), 128)
            upstream = gate[:, cols].astype(jnp.float32) * cot[:, cols].astype(jnp.float32)
            corr = flat[lane, pl.ds(place(row), shards, stride=rows), :]
            gsig_ref[:, cols] = (corr + skip * upstream).astype(jnp.bfloat16)
        return carry

    lax.fori_loop(0, rows, finish_corr, 0, unroll=8)
    for at in range(quarter):
        give(at, True)
    for at in range(quarter):
        take(at)
    scale = 1.0 / math.sqrt(SEQ)
    for group in range(own):
        total = trecv[group].astype(jnp.float32)
        for at in range(own + group, quarter, own):
            total = total + trecv[at].astype(jnp.float32)
        for lane in range(N2 // 128):
            flat[lane, group * rows : (group + 1) * rows, :] = total[:, lane * 128 : (lane + 1) * 128] * scale

    def finish_taps(row, carry):
        for lane in range(N2 // 128):
            cols = pl.ds(pl.multiple_of(row * N2 + lane * 128, 128), 128)
            gtaps_ref[:, cols] = flat[lane, pl.ds(place(row), own, stride=rows), :]
        return carry

    lax.fori_loop(0, rows, finish_taps, 0, unroll=8)
    drain(1, hsend, hgrid.at[lo])
    drain(0, send.at[0], recv.at[0])
    drain(2, send.at[1], recv.at[1])
    for step in range(1, tiles):
        taps_columns(step).wait_send()
        tap_terms(step).wait_send()
    drain(3, ysend.at[0], yrecv.at[0])
    drain(4, ysend.at[1], yrecv.at[1])


def emit(*refs):
    copies = [pltpu.make_async_copy(refs[at], refs[4 + at], refs[8].at[at]) for at in range(4)]
    for copy in copies:
        copy.start()
    for copy in copies:
        copy.wait()


def body(shards, chs, signal, gate, cotangent, skip_gain, filter_taps):
    channels, positions = signal.shape
    rows = positions // N2
    own = shards // chs
    block = 128
    bf16, f32 = jnp.bfloat16, jnp.float32
    hbm = pl.BlockSpec(memory_space=pl.ANY)
    vmem = pl.BlockSpec(memory_space=pltpu.VMEM)
    operands = signal, gate, cotangent, skip_gain, filter_taps, *tables()
    results = pl.pallas_call(
        functools.partial(kernel, shards, chs, rows, block),
        out_shape=[jax.ShapeDtypeStruct((channels, positions), bf16)] * 3
        + [jax.ShapeDtypeStruct((own, positions), f32)],
        in_specs=[hbm] * 11,
        out_specs=[vmem] * 4,
        scratch_shapes=[
            pltpu.VMEM((channels, positions), bf16),
            pltpu.VMEM((channels, positions), bf16),
            pltpu.VMEM((channels, positions), bf16),
            pltpu.SMEM((channels,), f32),
            pltpu.VMEM((channels, positions), f32),
            pltpu.VMEM((2, HALF, HALF // 2), bf16),
            pltpu.VMEM((N2, N2), bf16),
            pltpu.VMEM((N2, N2), bf16),
            pltpu.VMEM((2, HALF // 2, HALF), bf16),
            pltpu.VMEM((HALF, N2), f32),
            pltpu.VMEM((HALF, N2), f32),
            pltpu.VMEM((N2 // 128, HALF, 128), f32),
            pltpu.VMEM((2, shards, rows, N2), bf16),
            pltpu.VMEM((2, shards, rows, N2), bf16),
            pltpu.VMEM((shards, rows, 128), bf16),
            pltpu.VMEM((N2 // 128, shards, rows, 128), bf16),
            pltpu.VMEM((3, 2, HALF, N2), f32),
            pltpu.VMEM((HALF // 2 // block, 4, block, N2), bf16),
            pltpu.VMEM((2, HALF, N2), bf16),
            pltpu.VMEM((3, shards, rows, N2), bf16),
            pltpu.VMEM((2, shards, rows, N2), bf16),
            pltpu.VMEM((N2 // 128, shards * 128 // N2, rows, N2), bf16),
            pltpu.VMEM((shards * 128 // N2, rows, N2), bf16),
            pltpu.VMEM((shards * 128 // N2, rows, N2), bf16),
            pltpu.SemaphoreType.DMA((11,)),
            pltpu.SemaphoreType.DMA((6, shards)),
            pltpu.SemaphoreType.DMA((6, shards)),
            pltpu.SemaphoreType.DMA((2, N2 // 128)),
            pltpu.SemaphoreType.DMA((2, N2 // 128)),
        ],
        compiler_params=pltpu.CompilerParams(
            collective_id=0, has_side_effects=True, vmem_limit_bytes=48 * 1024 * 1024
        ),
    )(*[pltpu.with_memory_space_constraint(operand, pltpu.HBM) for operand in operands])
    return pl.pallas_call(
        emit,
        out_shape=[jax.ShapeDtypeStruct(result.shape, result.dtype) for result in results],
        in_specs=[hbm] * 4,
        out_specs=[hbm] * 4,
        scratch_shapes=[pltpu.SemaphoreType.DMA((4,))],
        compiler_params=pltpu.CompilerParams(vmem_limit_bytes=1024 * 1024),
    )(*results)


def solution(mesh):
    return jax.shard_map(
        functools.partial(body, mesh.shape["ctx"], mesh.shape["ch"]),
        mesh=mesh,
        in_specs=(P("ch", "ctx"), P("ch", "ctx"), P("ch", "ctx"), P("ch"), P(None, "ctx")),
        out_specs=(P("ch", "ctx"), P("ch", "ctx"), P("ch", "ctx"), P("ch", "ctx")),
        check_vma=False,
    )
```

```python
import functools
import math

import jax
import jax.numpy as jnp
import numpy as np
from jax import lax
from jax.experimental import pallas as pl
from jax.experimental.pallas import tpu as pltpu
from jax.sharding import PartitionSpec as P

N1 = 1024
N2 = 512
SEQ = 262144
HALF = N1 // 2
POINTS = N1 * N2
MESH = pl.DeviceIdType.MESH


def tables():
    quart, pair = HALF // 2, N2 // 2
    k1 = np.arange(quart, dtype=np.int64)
    n1 = np.arange(HALF, dtype=np.int64)
    n2 = np.arange(N2, dtype=np.int64)
    rows = np.concatenate([k1, HALF - 1 - k1])
    ang_a = ((2 * k1 + 1)[:, None] * n1[None, :] % (2 * N1)) * (math.pi / N1)
    ang_b = (n2[:, None] * n2[None, : pair + 1] % N2) * (2.0 * math.pi / N2)
    ang_t = ((2 * rows + 1)[:, None] * n2[None, :] % (2 * POINTS)) * (math.pi / POINTS)
    first = np.concatenate([np.cos(ang_a), -np.sin(ang_a)], axis=0)
    first = np.stack([first[:, 0::2], first[:, 1::2]])
    cos_b, sin_b = np.cos(ang_b), np.sin(ang_b)
    second = np.concatenate([cos_b[:, :pair], cos_b[:, pair:], sin_b[:, 1:pair]], axis=1)
    half = lambda a: jnp.asarray(np.ascontiguousarray(a).astype(np.float32)).astype(jnp.bfloat16)
    full = lambda a: jnp.asarray(a.astype(np.float32))
    return (
        half(first), half(second), half(second.T), half(2.0 / POINTS * first.transpose(0, 2, 1)),
        full(np.cos(ang_t)), full(np.sin(ang_t)),
    )


def dot(a, b):
    return jnp.dot(a, b, preferred_element_type=jnp.float32)


def kernel(
    shards, chs, rows, block,
    sig_hbm, gate_hbm, cot_hbm, gain_hbm, taps_hbm, first_hbm, second_hbm, under_hbm, back_hbm, twc_hbm, tws_hbm,
    out_ref, ggate_ref, gsig_ref, gtaps_ref,
    sig, gate, cot, gain, taps, first, second, under, back, twc, tws,
    flat, send, recv, hsend, hgrid, spec, both, stack, ysend, yrecv, tparts, tsend, trecv,
    load_sem, send_sem, recv_sem, share_send, share_recv, total_send, total_recv, ready,
):
    me = lax.axis_index("ctx")
    ch = lax.axis_index("ch")
    own = shards // chs
    tiles = N2 // 128
    quarter = shards // tiles
    hi, lo = ch // tiles, lax.rem(ch, tiles)

    loads = [
        pltpu.make_async_copy(src, dst, load_sem.at[i])
        for i, (src, dst) in enumerate(
            [(taps_hbm, taps), (sig_hbm, sig), (gate_hbm, gate), (cot_hbm, cot), (first_hbm, first),
             (twc_hbm, twc), (tws_hbm, tws), (second_hbm, second), (under_hbm, under), (back_hbm, back), (gain_hbm, gain)]
        )
    ]
    for load in loads:
        load.start()

    barrier = pltpu.get_barrier_semaphore()

    def greet_ctx(step, carry):
        pl.semaphore_signal(barrier, inc=1, device_id={"ctx": lax.rem(me + step, shards)}, device_id_type=MESH)
        return carry

    lax.fori_loop(1, shards, greet_ctx, 0)

    def is_self(peer_ctx, peer_ch):
        return jnp.logical_and(peer_ctx == me, peer_ch == ch)

    owner = me // own

    def source(at):
        return own * ch + at % own, at // own * tiles + me // quarter

    def signal(sem, condition, device):
        @pl.when(condition)
        def _():
            pl.semaphore_signal(sem, inc=1, device_id=device, device_id_type=MESH)

    for step in range(1, tiles):
        peer = lax.rem(lo + step, tiles)
        signal(barrier, peer > lo, {"ch": hi * tiles + peer})
    for at in range(quarter):
        peer_ctx, peer_ch = source(at)
        signal(barrier, peer_ch > ch, {"ctx": peer_ctx, "ch": peer_ch})
        signal(barrier, owner > ch, {"ctx": lo * quarter + at, "ch": owner})
    awaited = shards - 1 + lo + jnp.where(owner < ch, quarter, 0)
    for at in range(0, quarter, own):
        awaited = awaited + jnp.where(source(at)[1] < ch, own, 0)

    def answer():
        for step in range(1, tiles):
            peer = lax.rem(lo + step, tiles)
            signal(ready.at[0], peer < lo, {"ch": hi * tiles + peer})
        for at in range(quarter):
            peer_ctx, peer_ch = source(at)
            signal(ready.at[1], peer_ch < ch, {"ctx": peer_ctx, "ch": peer_ch})

    def place(row):
        return row // 2 + lax.rem(row, 2) * (rows // 2)

    def spread(which, value_at):
        def one(row, carry):
            for lane in range(N2 // 128):
                cols = pl.ds(pl.multiple_of(row * N2 + lane * 128, 128), 128)
                flat[lane, pl.ds(place(row), shards, stride=rows), :] = value_at(cols)
            return carry

        lax.fori_loop(0, rows, one, 0, unroll=8)

        def cast(at, carry):
            here = pl.ds(pl.multiple_of(at * rows, rows), rows)
            for lane in range(N2 // 128):
                send[which, at, :, lane * 128 : (lane + 1) * 128] = flat[lane, here, :].astype(jnp.bfloat16)
            return carry

        lax.fori_loop(0, shards, cast, 0, unroll=4)

    def remote(src, dst, which, device):
        return pltpu.make_async_remote_copy(
            src_ref=src, dst_ref=dst, send_sem=send_sem.at[which], recv_sem=recv_sem.at[which],
            device_id=device, device_id_type=MESH,
        )

    def peer_of(step):
        return lax.rem(me + step, shards)

    def each(first, last, action):
        def one(step, carry):
            action(step)
            return carry

        lax.fori_loop(first, last, one, 0, unroll=True)

    def exchange(which, src, dst):
        def one(step):
            peer = peer_of(step)
            remote(src.at[peer], dst.at[me], which, {"ctx": peer}).start()

        each(1, shards, one)
        pltpu.make_async_copy(src.at[me], dst.at[me], recv_sem.at[which]).start()

    def arrive(which, dst):
        pltpu.make_async_copy(dst, dst, recv_sem.at[which]).wait()

    def drain(which, src):
        sent = src.at[1:shards]
        pltpu.make_async_copy(sent, sent, send_sem.at[which]).wait()

    quart, pair = HALF // 2, N2 // 2
    edge = lax.broadcasted_iota(jnp.int32, (block, pair), 1) == 0

    def forward(which, load_grid):
        for at in range(quart // block):
            here = slice(at * block, (at + 1) * block)
            there = slice(quart + at * block, quart + (at + 1) * block)
            even, odd = load_grid()
            e_re, o_re = dot(first[0, here, :], even), dot(first[1, here, :], odd)
            e_im, o_im = dot(first[0, there, :], even), dot(first[1, there, :], odd)
            for part, rows_at, re, im in (
                (0, here, e_re + o_re, e_im + o_im), (1, there, e_re - o_re, o_im - e_im)
            ):
                cos, sin = twc[rows_at, :], tws[rows_at, :]
                both[at, part] = (re * cos + im * sin).astype(jnp.bfloat16)
                both[at, 2 + part] = (im * cos - re * sin).astype(jnp.bfloat16)
            summed = dot(both[at].reshape(4 * block, N2), second[...]).reshape(4, block, N2)
            for part, rows_at in ((0, here), (1, there)):
                r_c, r_s = summed[part][:, :pair], summed[part][:, pair:]
                i_c, i_s = summed[2 + part][:, :pair], summed[2 + part][:, pair:]
                spec[which, 0, rows_at, :pair] = jnp.where(edge, r_c, r_c + i_s)
                spec[which, 0, rows_at, pair:] = jnp.where(edge, r_s, r_c - i_s)
                spec[which, 1, rows_at, :pair] = jnp.where(edge, i_c, i_c - r_s)
                spec[which, 1, rows_at, pair:] = jnp.where(edge, i_s, i_c + r_s)

    def product(left, right, conj, rows_at, cols):
        l_re, l_im = spec[left, 0, rows_at, cols], spec[left, 1, rows_at, cols]
        r_re, r_im = spec[right, 0, rows_at, cols], spec[right, 1, rows_at, cols]
        if conj:
            return l_re * r_re + l_im * r_im, l_im * r_re - l_re * r_im
        return l_re * r_re - l_im * r_im, l_re * r_im + l_im * r_re

    def inverse(slot, left, right, conj):
        for at in range(quart // block):
            here = slice(at * block, (at + 1) * block)
            there = slice(quart + at * block, quart + (at + 1) * block)
            for part, rows_at in ((0, here), (1, there)):
                lo_re, lo_im = product(left, right, conj, rows_at, slice(0, pair))
                hi_re, hi_im = product(left, right, conj, rows_at, slice(pair, N2))
                both[at, part, :, :pair] = jnp.where(edge, lo_re, lo_re + hi_re).astype(jnp.bfloat16)
                both[at, part, :, pair:] = jnp.where(edge, hi_re, hi_im - lo_im).astype(jnp.bfloat16)
                both[at, 2 + part, :, :pair] = jnp.where(edge, lo_im, lo_im + hi_im).astype(jnp.bfloat16)
                both[at, 2 + part, :, pair:] = jnp.where(edge, hi_im, lo_re - hi_re).astype(jnp.bfloat16)
            summed = dot(both[at].reshape(4 * block, N2), under[...]).reshape(4, block, N2)
            twisted = []
            for part, rows_at in ((0, here), (1, there)):
                cos, sin = twc[rows_at, :], tws[rows_at, :]
                re, im = summed[part], summed[2 + part]
                twisted.append((re * cos - im * sin, re * sin + im * cos))
            (lo_re, lo_im), (hi_re, hi_im) = twisted
            stack[0, here, :] = (lo_re + hi_re).astype(jnp.bfloat16)
            stack[0, there, :] = (lo_im - hi_im).astype(jnp.bfloat16)
            stack[1, here, :] = (lo_re - hi_re).astype(jnp.bfloat16)
            stack[1, there, :] = (lo_im + hi_im).astype(jnp.bfloat16)
        for odd in range(2):
            value = dot(back[odd], stack[odd]).astype(jnp.bfloat16)
            ysend[slot, :, odd * (rows // 2) : (odd + 1) * (rows // 2)] = value.reshape(shards, rows // 2, N2)

    def share(step):
        return lax.rem(lo + step, tiles)

    def taps_columns(at):
        peer = hi * tiles + lax.rem(lo + (1, tiles - 1)[at], tiles)
        return pltpu.make_async_remote_copy(
            src_ref=hgrid.at[at], dst_ref=hgrid.at[3 - at], send_sem=share_send.at[0, at],
            recv_sem=share_recv.at[0, at], device_id={"ch": peer}, device_id_type=MESH,
        )

    def taps_out(step):
        peer = peer_of(step)
        remote(hsend.at[:, peer], hgrid.at[0:2, me], 1, {"ctx": peer}).start()

    def tap_terms(step):
        return pltpu.make_async_remote_copy(
            src_ref=ysend.at[2, pl.ds(share(step) * quarter, quarter)], dst_ref=tparts.at[step],
            send_sem=share_send.at[1, step], recv_sem=share_recv.at[1, step],
            device_id={"ch": hi * tiles + share(step)}, device_id_type=MESH,
        )

    loads[0].wait()

    def column(row, carry):
        for at in range(2):
            cols = pl.ds(pl.multiple_of(row * N2 + lax.rem(lo + at, tiles) * 128, 128), 128)
            flat[at, pl.ds(place(row), shards, stride=rows), :] = taps[:, cols]
        return carry

    lax.fori_loop(0, rows, column, 0, unroll=8)

    def cast_column(at, carry):
        for part in range(2):
            hsend[part, at] = flat[part, pl.ds(pl.multiple_of(at * rows, rows), rows), :].astype(jnp.bfloat16)
        return carry

    lax.fori_loop(0, shards, cast_column, 0, unroll=4)
    pl.semaphore_wait(barrier, awaited)
    each(1, shards, taps_out)
    pltpu.make_async_copy(hsend.at[:, me], hgrid.at[0:2, me], recv_sem.at[1]).start()
    loads[1].wait()
    spread(0, lambda cols: sig[:, cols].astype(jnp.float32))
    exchange(0, send.at[0], recv.at[0])
    answer()
    arrive(1, hgrid.at[0:2])

    @pl.when(lo < tiles - 1)
    def _():
        pl.semaphore_wait(ready.at[0], tiles - 1 - lo)

    for at in range(2):
        taps_columns(at).start()

    loads[2].wait()
    loads[3].wait()
    spread(1, lambda cols: gate[:, cols].astype(jnp.float32) * cot[:, cols].astype(jnp.float32))
    exchange(2, send.at[1], recv.at[1])
    for load in loads[4:]:
        load.wait()
    def arrived(which):
        return [
            recv[which, :, odd * (rows // 2) : (odd + 1) * (rows // 2), :].reshape(HALF // 2, N2) for odd in range(2)
        ]

    def arrived_taps():
        tile = lambda at, odd: hgrid[lax.rem(at + tiles - lo, tiles), :, odd * (rows // 2) : (odd + 1) * (rows // 2), :].reshape(HALF // 2, 128)
        return [jnp.concatenate([tile(at, odd) for at in range(tiles)], axis=1) for odd in range(2)]

    for at in range(2):
        taps_columns(at).wait_recv()
    forward(1, arrived_taps)
    arrive(0, recv.at[0])
    forward(0, lambda: arrived(0))
    inverse(0, 0, 1, False)
    exchange(3, ysend.at[0], yrecv.at[0])
    arrive(2, recv.at[1])
    forward(2, lambda: arrived(1))
    inverse(2, 2, 0, True)
    for step in range(1, tiles):
        tap_terms(step).start()
    inverse(1, 2, 1, True)
    exchange(4, ysend.at[1], yrecv.at[1])

    sent = hsend.at[:, 1:shards]
    pltpu.make_async_copy(sent, sent, send_sem.at[1]).wait()
    drain(0, send.at[0])
    drain(2, send.at[1])
    for at in range(2):
        taps_columns(at).wait_send()
    def gather(slot):
        def one(at, carry):
            here = pl.ds(pl.multiple_of(at * rows, rows), rows)
            for lane in range(N2 // 128):
                flat[lane, here, :] = yrecv[slot, at, :, lane * 128 : (lane + 1) * 128].astype(jnp.float32)
            return carry

        lax.fori_loop(0, shards, one, 0, unroll=4)

    channel = lax.broadcasted_iota(jnp.int32, (shards, 128), 0)
    skip = jnp.zeros((shards, 128), jnp.float32)
    for at in range(shards):
        skip = jnp.where(channel == at, gain[at], skip)
    arrive(3, yrecv.at[0])
    gather(0)

    def finish_conv(row, carry):
        for lane in range(N2 // 128):
            cols = pl.ds(pl.multiple_of(row * N2 + lane * 128, 128), 128)
            mixed = flat[lane, pl.ds(place(row), shards, stride=rows), :] + skip * sig[:, cols].astype(jnp.float32)
            out_ref[:, cols] = (gate[:, cols].astype(jnp.float32) * mixed).astype(jnp.bfloat16)
            ggate_ref[:, cols] = (cot[:, cols].astype(jnp.float32) * mixed).astype(jnp.bfloat16)
        return carry

    lax.fori_loop(0, rows, finish_conv, 0, unroll=8)
    for step in range(1, tiles):
        tap_terms(step).wait_recv()
    for at in range(quarter):
        total = ysend[2, lo * quarter + at].astype(jnp.float32)
        for step in range(1, tiles):
            total = total + tparts[step, at].astype(jnp.float32)
        tsend[at] = total.astype(jnp.bfloat16)

    for step in range(1, tiles):
        tap_terms(step).wait_send()
    slot = hi * own + lax.rem(me, own)

    def tap_total(at, device):
        return pltpu.make_async_remote_copy(
            src_ref=tsend.at[at], dst_ref=trecv.at[slot], send_sem=total_send.at[at], recv_sem=total_recv.at[slot],
            device_id=device, device_id_type=MESH,
        )

    def give(at, wait):
        peer = lo * quarter + at
        local = is_self(peer, owner)

        @pl.when(local)
        def _():
            copy = pltpu.make_async_copy(tsend.at[at], trecv.at[slot], total_recv.at[slot])
            copy.wait() if wait else copy.start()

        @pl.when(jnp.logical_not(local))
        def _():
            copy = tap_total(at, {"ctx": peer, "ch": owner})
            copy.wait_send() if wait else copy.start()

    def take(at):
        peer_ctx, peer_ch = source(at)

        @pl.when(jnp.logical_not(is_self(peer_ctx, peer_ch)))
        def _():
            pltpu.make_async_copy(tsend.at[0], trecv.at[at], total_recv.at[at]).wait()


    @pl.when(owner > ch)
    def _():
        pl.semaphore_wait(ready.at[1], quarter)

    for at in range(quarter):
        give(at, False)
    drain(3, ysend.at[0])
    arrive(4, yrecv.at[1])
    gather(1)

    def finish_corr(row, carry):
        for lane in range(N2 // 128):
            cols = pl.ds(pl.multiple_of(row * N2 + lane * 128, 128), 128)
            upstream = gate[:, cols].astype(jnp.float32) * cot[:, cols].astype(jnp.float32)
            corr = flat[lane, pl.ds(place(row), shards, stride=rows), :]
            gsig_ref[:, cols] = (corr + skip * upstream).astype(jnp.bfloat16)
        return carry

    lax.fori_loop(0, rows, finish_corr, 0, unroll=8)
    for at in range(quarter):
        give(at, True)
    for at in range(quarter):
        take(at)
    scale = 1.0 / math.sqrt(SEQ)
    for group in range(own):
        total = trecv[group].astype(jnp.float32)
        for at in range(own + group, quarter, own):
            total = total + trecv[at].astype(jnp.float32)
        for lane in range(N2 // 128):
            flat[lane, group * rows : (group + 1) * rows, :] = total[:, lane * 128 : (lane + 1) * 128] * scale

    def finish_taps(row, carry):
        for lane in range(N2 // 128):
            cols = pl.ds(pl.multiple_of(row * N2 + lane * 128, 128), 128)
            gtaps_ref[:, cols] = flat[lane, pl.ds(place(row), own, stride=rows), :]
        return carry

    lax.fori_loop(0, rows, finish_taps, 0, unroll=8)
    drain(4, ysend.at[1])


def emit(*refs):
    copies = [pltpu.make_async_copy(refs[at], refs[4 + at], refs[8].at[at]) for at in range(4)]
    for copy in copies:
        copy.start()
    for copy in copies:
        copy.wait()


def body(shards, chs, signal, gate, cotangent, skip_gain, filter_taps):
    channels, positions = signal.shape
    rows = positions // N2
    own = shards // chs
    block = 128
    bf16, f32 = jnp.bfloat16, jnp.float32
    hbm = pl.BlockSpec(memory_space=pl.ANY)
    vmem = pl.BlockSpec(memory_space=pltpu.VMEM)
    operands = signal, gate, cotangent, skip_gain, filter_taps, *tables()
    results = pl.pallas_call(
        functools.partial(kernel, shards, chs, rows, block),
        out_shape=[jax.ShapeDtypeStruct((channels, positions), bf16)] * 3
        + [jax.ShapeDtypeStruct((own, positions), f32)],
        in_specs=[hbm] * 11,
        out_specs=[vmem] * 4,
        scratch_shapes=[
            pltpu.VMEM((channels, positions), bf16),
            pltpu.VMEM((channels, positions), bf16),
            pltpu.VMEM((channels, positions), bf16),
            pltpu.SMEM((channels,), f32),
            pltpu.VMEM((channels, positions), f32),
            pltpu.VMEM((2, HALF, HALF // 2), bf16),
            pltpu.VMEM((N2, N2), bf16),
            pltpu.VMEM((N2, N2), bf16),
            pltpu.VMEM((2, HALF // 2, HALF), bf16),
            pltpu.VMEM((HALF, N2), f32),
            pltpu.VMEM((HALF, N2), f32),
            pltpu.VMEM((N2 // 128, HALF, 128), f32),
            pltpu.VMEM((2, shards, rows, N2), bf16),
            pltpu.VMEM((2, shards, rows, N2), bf16),
            pltpu.VMEM((2, shards, rows, 128), bf16),
            pltpu.VMEM((N2 // 128, shards, rows, 128), bf16),
            pltpu.VMEM((3, 2, HALF, N2), f32),
            pltpu.VMEM((HALF // 2 // block, 4, block, N2), bf16),
            pltpu.VMEM((2, HALF, N2), bf16),
            pltpu.VMEM((3, shards, rows, N2), bf16),
            pltpu.VMEM((2, shards, rows, N2), bf16),
            pltpu.VMEM((N2 // 128, shards * 128 // N2, rows, N2), bf16),
            pltpu.VMEM((shards * 128 // N2, rows, N2), bf16),
            pltpu.VMEM((shards * 128 // N2, rows, N2), bf16),
            pltpu.SemaphoreType.DMA((11,)),
            pltpu.SemaphoreType.DMA((5,)),
            pltpu.SemaphoreType.DMA((5,)),
            pltpu.SemaphoreType.DMA((2, N2 // 128)),
            pltpu.SemaphoreType.DMA((2, N2 // 128)),
            pltpu.SemaphoreType.DMA((shards * 128 // N2,)),
            pltpu.SemaphoreType.DMA((shards * 128 // N2,)),
            pltpu.SemaphoreType.REGULAR((2,)),
        ],
        compiler_params=pltpu.CompilerParams(
            collective_id=0, has_side_effects=True, vmem_limit_bytes=48 * 1024 * 1024
        ),
    )(*[pltpu.with_memory_space_constraint(operand, pltpu.HBM) for operand in operands])
    return pl.pallas_call(
        emit,
        out_shape=[jax.ShapeDtypeStruct(result.shape, result.dtype) for result in results],
        in_specs=[hbm] * 4,
        out_specs=[hbm] * 4,
        scratch_shapes=[pltpu.SemaphoreType.DMA((4,))],
        compiler_params=pltpu.CompilerParams(vmem_limit_bytes=1024 * 1024),
    )(*results)


def solution(mesh):
    return jax.shard_map(
        functools.partial(body, mesh.shape["ctx"], mesh.shape["ch"]),
        mesh=mesh,
        in_specs=(P("ch", "ctx"), P("ch", "ctx"), P("ch", "ctx"), P("ch"), P(None, "ctx")),
        out_specs=(P("ch", "ctx"), P("ch", "ctx"), P("ch", "ctx"), P("ch", "ctx")),
        check_vma=False,
    )
```

```python
import functools
import math

import jax
import jax.numpy as jnp
import numpy as np
from jax import lax
from jax.experimental import pallas as pl
from jax.experimental.pallas import tpu as pltpu
from jax.sharding import PartitionSpec as P

N1 = 1024
N2 = 512
SEQ = 262144
HALF = N1 // 2
POINTS = N1 * N2
MESH = pl.DeviceIdType.MESH


def tables():
    quart, pair = HALF // 2, N2 // 2
    k1 = np.arange(quart, dtype=np.int64)
    n1 = np.arange(HALF, dtype=np.int64)
    n2 = np.arange(N2, dtype=np.int64)
    rows = np.concatenate([k1, HALF - 1 - k1])
    ang_a = ((2 * k1 + 1)[:, None] * n1[None, :] % (2 * N1)) * (math.pi / N1)
    ang_b = (n2[:, None] * n2[None, : pair + 1] % N2) * (2.0 * math.pi / N2)
    ang_t = ((2 * rows + 1)[:, None] * n2[None, :] % (2 * POINTS)) * (math.pi / POINTS)
    first = np.concatenate([np.cos(ang_a), -np.sin(ang_a)], axis=0)
    first = np.stack([first[:, 0::2], first[:, 1::2]])
    cos_b, sin_b = np.cos(ang_b), np.sin(ang_b)
    second = np.concatenate([cos_b[:, :pair], cos_b[:, pair:], sin_b[:, 1:pair]], axis=1)
    half = lambda a: jnp.asarray(np.ascontiguousarray(a).astype(np.float32)).astype(jnp.bfloat16)
    full = lambda a: jnp.asarray(a.astype(np.float32))
    return (
        half(first), half(second), half(second.T), half(2.0 / POINTS * first.transpose(0, 2, 1)),
        full(np.cos(ang_t)), full(np.sin(ang_t)),
    )


def dot(a, b):
    return jnp.dot(a, b, preferred_element_type=jnp.float32)


def kernel(
    shards, chs, rows, block,
    sig_hbm, gate_hbm, cot_hbm, gain_hbm, taps_hbm, first_hbm, second_hbm, under_hbm, back_hbm, twc_hbm, tws_hbm,
    out_ref, ggate_ref, gsig_ref, gtaps_ref,
    sig, gate, cot, gain, taps, first, second, under, back, twc, tws,
    flat, send, recv, hsend, hgrid, spec, both, stack, ysend, yrecv, tparts, tsend, trecv,
    load_sem, send_sem, recv_sem, share_send, share_recv, total_send, total_recv, ready,
):
    me = lax.axis_index("ctx")
    ch = lax.axis_index("ch")
    own = shards // chs
    tiles = N2 // 128
    quarter = shards // tiles
    hi, lo = ch // tiles, lax.rem(ch, tiles)

    loads = [
        pltpu.make_async_copy(src, dst, load_sem.at[i])
        for i, (src, dst) in enumerate(
            [(taps_hbm, taps), (sig_hbm, sig), (gate_hbm, gate), (cot_hbm, cot), (first_hbm, first),
             (twc_hbm, twc), (tws_hbm, tws), (second_hbm, second), (under_hbm, under), (back_hbm, back), (gain_hbm, gain)]
        )
    ]
    for load in loads:
        load.start()

    barrier = pltpu.get_barrier_semaphore()

    def greet_ctx(step, carry):
        pl.semaphore_signal(barrier, inc=1, device_id={"ctx": lax.rem(me + step, shards)}, device_id_type=MESH)
        return carry

    lax.fori_loop(1, shards, greet_ctx, 0)

    def is_self(peer_ctx, peer_ch):
        return jnp.logical_and(peer_ctx == me, peer_ch == ch)

    owner = me // own

    def source(at):
        return own * ch + at % own, at // own * tiles + me // quarter

    def signal(sem, condition, device):
        @pl.when(condition)
        def _():
            pl.semaphore_signal(sem, inc=1, device_id=device, device_id_type=MESH)

    for step in range(1, tiles):
        peer = lax.rem(lo + step, tiles)
        signal(barrier, peer > lo, {"ch": hi * tiles + peer})
    for at in range(quarter):
        peer_ctx, peer_ch = source(at)
        signal(barrier, peer_ch > ch, {"ctx": peer_ctx, "ch": peer_ch})
        signal(barrier, owner > ch, {"ctx": lo * quarter + at, "ch": owner})
    awaited = shards - 1 + lo + jnp.where(owner < ch, quarter, 0)
    for at in range(0, quarter, own):
        awaited = awaited + jnp.where(source(at)[1] < ch, own, 0)

    def answer():
        for step in range(1, tiles):
            peer = lax.rem(lo + step, tiles)
            signal(ready.at[0], peer < lo, {"ch": hi * tiles + peer})
        for at in range(quarter):
            peer_ctx, peer_ch = source(at)
            signal(ready.at[1], peer_ch < ch, {"ctx": peer_ctx, "ch": peer_ch})

    def place(row):
        return row // 2 + lax.rem(row, 2) * (rows // 2)

    def spread(which, value_at):
        def one(row, carry):
            for lane in range(N2 // 128):
                cols = pl.ds(pl.multiple_of(row * N2 + lane * 128, 128), 128)
                flat[lane, pl.ds(place(row), shards, stride=rows), :] = value_at(cols)
            return carry

        lax.fori_loop(0, rows, one, 0, unroll=8)

        def cast(at, carry):
            here = pl.ds(pl.multiple_of(at * rows, rows), rows)
            for lane in range(N2 // 128):
                send[which, at, :, lane * 128 : (lane + 1) * 128] = flat[lane, here, :].astype(jnp.bfloat16)
            return carry

        lax.fori_loop(0, shards, cast, 0, unroll=4)

    def remote(src, dst, which, device):
        return pltpu.make_async_remote_copy(
            src_ref=src, dst_ref=dst, send_sem=send_sem.at[which], recv_sem=recv_sem.at[which],
            device_id=device, device_id_type=MESH,
        )

    def peer_of(step):
        return lax.rem(me + step, shards)

    def each(first, last, action):
        def one(step, carry):
            action(step)
            return carry

        lax.fori_loop(first, last, one, 0, unroll=True)

    def exchange(which, src, dst):
        def one(step):
            peer = peer_of(step)
            remote(src.at[peer], dst.at[me], which, {"ctx": peer}).start()

        each(1, shards, one)
        pltpu.make_async_copy(src.at[me], dst.at[me], recv_sem.at[which]).start()

    def arrive(which, dst):
        pltpu.make_async_copy(dst, dst, recv_sem.at[which]).wait()

    def drain(which, src):
        sent = src.at[1:shards]
        pltpu.make_async_copy(sent, sent, send_sem.at[which]).wait()

    quart, pair = HALF // 2, N2 // 2
    edge = lax.broadcasted_iota(jnp.int32, (block, pair), 1) == 0

    def forward(which, load_grid):
        for at in range(quart // block):
            here = slice(at * block, (at + 1) * block)
            there = slice(quart + at * block, quart + (at + 1) * block)
            even, odd = load_grid()
            e_re, o_re = dot(first[0, here, :], even), dot(first[1, here, :], odd)
            e_im, o_im = dot(first[0, there, :], even), dot(first[1, there, :], odd)
            for part, rows_at, re, im in (
                (0, here, e_re + o_re, e_im + o_im), (1, there, e_re - o_re, o_im - e_im)
            ):
                cos, sin = twc[rows_at, :], tws[rows_at, :]
                both[at, part] = (re * cos + im * sin).astype(jnp.bfloat16)
                both[at, 2 + part] = (im * cos - re * sin).astype(jnp.bfloat16)
            summed = dot(both[at].reshape(4 * block, N2), second[...]).reshape(4, block, N2)
            for part, rows_at in ((0, here), (1, there)):
                r_c, r_s = summed[part][:, :pair], summed[part][:, pair:]
                i_c, i_s = summed[2 + part][:, :pair], summed[2 + part][:, pair:]
                spec[which, 0, rows_at, :pair] = jnp.where(edge, r_c, r_c + i_s)
                spec[which, 0, rows_at, pair:] = jnp.where(edge, r_s, r_c - i_s)
                spec[which, 1, rows_at, :pair] = jnp.where(edge, i_c, i_c - r_s)
                spec[which, 1, rows_at, pair:] = jnp.where(edge, i_s, i_c + r_s)

    def product(left, right, conj, rows_at, cols):
        l_re, l_im = spec[left, 0, rows_at, cols], spec[left, 1, rows_at, cols]
        r_re, r_im = spec[right, 0, rows_at, cols], spec[right, 1, rows_at, cols]
        if conj:
            return l_re * r_re + l_im * r_im, l_im * r_re - l_re * r_im
        return l_re * r_re - l_im * r_im, l_re * r_im + l_im * r_re

    def inverse(slot, left, right, conj):
        for at in range(quart // block):
            here = slice(at * block, (at + 1) * block)
            there = slice(quart + at * block, quart + (at + 1) * block)
            for part, rows_at in ((0, here), (1, there)):
                lo_re, lo_im = product(left, right, conj, rows_at, slice(0, pair))
                hi_re, hi_im = product(left, right, conj, rows_at, slice(pair, N2))
                both[at, part, :, :pair] = jnp.where(edge, lo_re, lo_re + hi_re).astype(jnp.bfloat16)
                both[at, part, :, pair:] = jnp.where(edge, hi_re, hi_im - lo_im).astype(jnp.bfloat16)
                both[at, 2 + part, :, :pair] = jnp.where(edge, lo_im, lo_im + hi_im).astype(jnp.bfloat16)
                both[at, 2 + part, :, pair:] = jnp.where(edge, hi_im, lo_re - hi_re).astype(jnp.bfloat16)
            summed = dot(both[at].reshape(4 * block, N2), under[...]).reshape(4, block, N2)
            twisted = []
            for part, rows_at in ((0, here), (1, there)):
                cos, sin = twc[rows_at, :], tws[rows_at, :]
                re, im = summed[part], summed[2 + part]
                twisted.append((re * cos - im * sin, re * sin + im * cos))
            (lo_re, lo_im), (hi_re, hi_im) = twisted
            stack[0, here, :] = (lo_re + hi_re).astype(jnp.bfloat16)
            stack[0, there, :] = (lo_im - hi_im).astype(jnp.bfloat16)
            stack[1, here, :] = (lo_re - hi_re).astype(jnp.bfloat16)
            stack[1, there, :] = (lo_im + hi_im).astype(jnp.bfloat16)
        for odd in range(2):
            value = dot(back[odd], stack[odd]).astype(jnp.bfloat16)
            ysend[slot, :, odd * (rows // 2) : (odd + 1) * (rows // 2)] = value.reshape(shards, rows // 2, N2)

    def share(step):
        return lax.rem(lo + step, tiles)

    def taps_columns(at):
        peer = hi * tiles + lax.rem(lo + (1, tiles - 1)[at], tiles)
        return pltpu.make_async_remote_copy(
            src_ref=hgrid.at[at], dst_ref=hgrid.at[3 - at], send_sem=share_send.at[0, at],
            recv_sem=share_recv.at[0, at], device_id={"ch": peer}, device_id_type=MESH,
        )

    def taps_out(step):
        peer = peer_of(step)
        remote(hsend.at[:, peer], hgrid.at[0:2, me], 1, {"ctx": peer}).start()

    def tap_terms(step):
        return pltpu.make_async_remote_copy(
            src_ref=ysend.at[2, pl.ds(share(step) * quarter, quarter)], dst_ref=tparts.at[step],
            send_sem=share_send.at[1, step], recv_sem=share_recv.at[1, step],
            device_id={"ch": hi * tiles + share(step)}, device_id_type=MESH,
        )

    def tap_term(step, at):
        return pltpu.make_async_remote_copy(
            src_ref=ysend.at[2, share(step) * quarter + at], dst_ref=tparts.at[step, at],
            send_sem=share_send.at[1, step], recv_sem=share_recv.at[1, step],
            device_id={"ch": hi * tiles + share(step)}, device_id_type=MESH,
        )

    loads[0].wait()

    def column(row, carry):
        for at in range(2):
            cols = pl.ds(pl.multiple_of(row * N2 + lax.rem(lo + at, tiles) * 128, 128), 128)
            flat[at, pl.ds(place(row), shards, stride=rows), :] = taps[:, cols]
        return carry

    lax.fori_loop(0, rows, column, 0, unroll=8)

    def cast_column(at, carry):
        for part in range(2):
            hsend[part, at] = flat[part, pl.ds(pl.multiple_of(at * rows, rows), rows), :].astype(jnp.bfloat16)
        return carry

    lax.fori_loop(0, shards, cast_column, 0, unroll=4)
    pl.semaphore_wait(barrier, awaited)
    each(1, shards, taps_out)
    pltpu.make_async_copy(hsend.at[:, me], hgrid.at[0:2, me], recv_sem.at[1]).start()
    loads[1].wait()
    spread(0, lambda cols: sig[:, cols].astype(jnp.float32))
    exchange(0, send.at[0], recv.at[0])
    answer()
    arrive(1, hgrid.at[0:2])

    @pl.when(lo < tiles - 1)
    def _():
        pl.semaphore_wait(ready.at[0], tiles - 1 - lo)

    for at in range(2):
        taps_columns(at).start()

    loads[2].wait()
    loads[3].wait()
    spread(1, lambda cols: gate[:, cols].astype(jnp.float32) * cot[:, cols].astype(jnp.float32))
    exchange(2, send.at[1], recv.at[1])
    for load in loads[4:]:
        load.wait()
    def arrived(which):
        return [
            recv[which, :, odd * (rows // 2) : (odd + 1) * (rows // 2), :].reshape(HALF // 2, N2) for odd in range(2)
        ]

    def arrived_taps():
        tile = lambda at, odd: hgrid[lax.rem(at + tiles - lo, tiles), :, odd * (rows // 2) : (odd + 1) * (rows // 2), :].reshape(HALF // 2, 128)
        return [jnp.concatenate([tile(at, odd) for at in range(tiles)], axis=1) for odd in range(2)]

    for at in range(2):
        taps_columns(at).wait_recv()
    forward(1, arrived_taps)
    arrive(0, recv.at[0])
    forward(0, lambda: arrived(0))
    inverse(0, 0, 1, False)
    exchange(3, ysend.at[0], yrecv.at[0])
    arrive(2, recv.at[1])
    forward(2, lambda: arrived(1))
    inverse(2, 2, 0, True)
    for at in range(quarter):
        for step in (2, 1, 3):
            tap_term(step, at).start()
    inverse(1, 2, 1, True)
    exchange(4, ysend.at[1], yrecv.at[1])

    sent = hsend.at[:, 1:shards]
    pltpu.make_async_copy(sent, sent, send_sem.at[1]).wait()
    drain(0, send.at[0])
    drain(2, send.at[1])
    for at in range(2):
        taps_columns(at).wait_send()
    def gather(slot):
        def one(at, carry):
            here = pl.ds(pl.multiple_of(at * rows, rows), rows)
            for lane in range(N2 // 128):
                flat[lane, here, :] = yrecv[slot, at, :, lane * 128 : (lane + 1) * 128].astype(jnp.float32)
            return carry

        lax.fori_loop(0, shards, one, 0, unroll=4)

    channel = lax.broadcasted_iota(jnp.int32, (shards, 128), 0)
    skip = jnp.zeros((shards, 128), jnp.float32)
    for at in range(shards):
        skip = jnp.where(channel == at, gain[at], skip)
    for step in range(1, tiles):
        tap_terms(step).wait_recv()
    slot = hi * own + lax.rem(me, own)

    def tap_total(at, device):
        return pltpu.make_async_remote_copy(
            src_ref=tsend.at[at], dst_ref=trecv.at[slot], send_sem=total_send.at[at], recv_sem=total_recv.at[slot],
            device_id=device, device_id_type=MESH,
        )

    def give(at, wait):
        peer = lo * quarter + at
        local = is_self(peer, owner)

        @pl.when(local)
        def _():
            copy = pltpu.make_async_copy(tsend.at[at], trecv.at[slot], total_recv.at[slot])
            copy.wait() if wait else copy.start()

        @pl.when(jnp.logical_not(local))
        def _():
            copy = tap_total(at, {"ctx": peer, "ch": owner})
            copy.wait_send() if wait else copy.start()

    def take(at):
        peer_ctx, peer_ch = source(at)

        @pl.when(jnp.logical_not(is_self(peer_ctx, peer_ch)))
        def _():
            pltpu.make_async_copy(tsend.at[0], trecv.at[at], total_recv.at[at]).wait()


    @pl.when(owner > ch)
    def _():
        pl.semaphore_wait(ready.at[1], quarter)

    for at in range(quarter):
        total = ysend[2, lo * quarter + at].astype(jnp.float32)
        for step in range(1, tiles):
            total = total + tparts[step, at].astype(jnp.float32)
        tsend[at] = total.astype(jnp.bfloat16)

        give(at, False)
    for step in range(1, tiles):
        tap_terms(step).wait_send()
    arrive(3, yrecv.at[0])
    gather(0)

    def finish_conv(row, carry):
        for lane in range(N2 // 128):
            cols = pl.ds(pl.multiple_of(row * N2 + lane * 128, 128), 128)
            mixed = flat[lane, pl.ds(place(row), shards, stride=rows), :] + skip * sig[:, cols].astype(jnp.float32)
            out_ref[:, cols] = (gate[:, cols].astype(jnp.float32) * mixed).astype(jnp.bfloat16)
            ggate_ref[:, cols] = (cot[:, cols].astype(jnp.float32) * mixed).astype(jnp.bfloat16)
        return carry

    lax.fori_loop(0, rows, finish_conv, 0, unroll=8)
    drain(3, ysend.at[0])
    arrive(4, yrecv.at[1])
    gather(1)

    def finish_corr(row, carry):
        for lane in range(N2 // 128):
            cols = pl.ds(pl.multiple_of(row * N2 + lane * 128, 128), 128)
            upstream = gate[:, cols].astype(jnp.float32) * cot[:, cols].astype(jnp.float32)
            corr = flat[lane, pl.ds(place(row), shards, stride=rows), :]
            gsig_ref[:, cols] = (corr + skip * upstream).astype(jnp.bfloat16)
        return carry

    lax.fori_loop(0, rows, finish_corr, 0, unroll=8)
    for at in range(quarter):
        give(at, True)
    for at in range(quarter):
        take(at)
    scale = 1.0 / math.sqrt(SEQ)
    for group in range(own):
        total = trecv[group].astype(jnp.float32)
        for at in range(own + group, quarter, own):
            total = total + trecv[at].astype(jnp.float32)
        for lane in range(N2 // 128):
            flat[lane, group * rows : (group + 1) * rows, :] = total[:, lane * 128 : (lane + 1) * 128] * scale

    def finish_taps(row, carry):
        for lane in range(N2 // 128):
            cols = pl.ds(pl.multiple_of(row * N2 + lane * 128, 128), 128)
            gtaps_ref[:, cols] = flat[lane, pl.ds(place(row), own, stride=rows), :]
        return carry

    lax.fori_loop(0, rows, finish_taps, 0, unroll=8)
    drain(4, ysend.at[1])


def emit(*refs):
    copies = [pltpu.make_async_copy(refs[at], refs[4 + at], refs[8].at[at]) for at in range(4)]
    for copy in copies:
        copy.start()
    for copy in copies:
        copy.wait()


def body(shards, chs, signal, gate, cotangent, skip_gain, filter_taps):
    channels, positions = signal.shape
    rows = positions // N2
    own = shards // chs
    block = 128
    bf16, f32 = jnp.bfloat16, jnp.float32
    hbm = pl.BlockSpec(memory_space=pl.ANY)
    vmem = pl.BlockSpec(memory_space=pltpu.VMEM)
    operands = signal, gate, cotangent, skip_gain, filter_taps, *tables()
    results = pl.pallas_call(
        functools.partial(kernel, shards, chs, rows, block),
        out_shape=[jax.ShapeDtypeStruct((channels, positions), bf16)] * 3
        + [jax.ShapeDtypeStruct((own, positions), f32)],
        in_specs=[hbm] * 11,
        out_specs=[vmem] * 4,
        scratch_shapes=[
            pltpu.VMEM((channels, positions), bf16),
            pltpu.VMEM((channels, positions), bf16),
            pltpu.VMEM((channels, positions), bf16),
            pltpu.SMEM((channels,), f32),
            pltpu.VMEM((channels, positions), f32),
            pltpu.VMEM((2, HALF, HALF // 2), bf16),
            pltpu.VMEM((N2, N2), bf16),
            pltpu.VMEM((N2, N2), bf16),
            pltpu.VMEM((2, HALF // 2, HALF), bf16),
            pltpu.VMEM((HALF, N2), f32),
            pltpu.VMEM((HALF, N2), f32),
            pltpu.VMEM((N2 // 128, HALF, 128), f32),
            pltpu.VMEM((2, shards, rows, N2), bf16),
            pltpu.VMEM((2, shards, rows, N2), bf16),
            pltpu.VMEM((2, shards, rows, 128), bf16),
            pltpu.VMEM((N2 // 128, shards, rows, 128), bf16),
            pltpu.VMEM((3, 2, HALF, N2), f32),
            pltpu.VMEM((HALF // 2 // block, 4, block, N2), bf16),
            pltpu.VMEM((2, HALF, N2), bf16),
            pltpu.VMEM((3, shards, rows, N2), bf16),
            pltpu.VMEM((2, shards, rows, N2), bf16),
            pltpu.VMEM((N2 // 128, shards * 128 // N2, rows, N2), bf16),
            pltpu.VMEM((shards * 128 // N2, rows, N2), bf16),
            pltpu.VMEM((shards * 128 // N2, rows, N2), bf16),
            pltpu.SemaphoreType.DMA((11,)),
            pltpu.SemaphoreType.DMA((5,)),
            pltpu.SemaphoreType.DMA((5,)),
            pltpu.SemaphoreType.DMA((2, N2 // 128)),
            pltpu.SemaphoreType.DMA((2, N2 // 128)),
            pltpu.SemaphoreType.DMA((shards * 128 // N2,)),
            pltpu.SemaphoreType.DMA((shards * 128 // N2,)),
            pltpu.SemaphoreType.REGULAR((2,)),
        ],
        compiler_params=pltpu.CompilerParams(
            collective_id=0, has_side_effects=True, vmem_limit_bytes=48 * 1024 * 1024
        ),
    )(*[pltpu.with_memory_space_constraint(operand, pltpu.HBM) for operand in operands])
    return pl.pallas_call(
        emit,
        out_shape=[jax.ShapeDtypeStruct(result.shape, result.dtype) for result in results],
        in_specs=[hbm] * 4,
        out_specs=[hbm] * 4,
        scratch_shapes=[pltpu.SemaphoreType.DMA((4,))],
        compiler_params=pltpu.CompilerParams(vmem_limit_bytes=1024 * 1024),
    )(*results)


def solution(mesh):
    return jax.shard_map(
        functools.partial(body, mesh.shape["ctx"], mesh.shape["ch"]),
        mesh=mesh,
        in_specs=(P("ch", "ctx"), P("ch", "ctx"), P("ch", "ctx"), P("ch"), P(None, "ctx")),
        out_specs=(P("ch", "ctx"), P("ch", "ctx"), P("ch", "ctx"), P("ch", "ctx")),
        check_vma=False,
    )
```

```python
import functools
import math

import jax
import jax.numpy as jnp
import numpy as np
from jax import lax
from jax.experimental import pallas as pl
from jax.experimental.pallas import tpu as pltpu
from jax.sharding import PartitionSpec as P

N1 = 1024
N2 = 512
SEQ = 262144
HALF = N1 // 2
POINTS = N1 * N2
BLOCK = 256
MESH = pl.DeviceIdType.MESH


def tables():
    quart, pair = HALF // 2, N2 // 2
    k1 = np.arange(quart, dtype=np.int64)
    n1 = np.arange(HALF, dtype=np.int64)
    n2 = np.arange(N2, dtype=np.int64)
    rows = np.concatenate([k1, HALF - 1 - k1])
    ang_a = ((2 * k1 + 1)[:, None] * n1[None, :] % (2 * N1)) * (math.pi / N1)
    ang_b = (n2[:, None] * n2[None, : pair + 1] % N2) * (2.0 * math.pi / N2)
    ang_t = ((2 * rows + 1)[:, None] * n2[None, :] % (2 * POINTS)) * (math.pi / POINTS)
    first = np.concatenate([np.cos(ang_a), -np.sin(ang_a)], axis=0)
    first = np.stack([first[:, 0::2], first[:, 1::2]])
    back_first = 2.0 / POINTS * first.transpose(0, 2, 1)
    first = first.reshape(2, 2, quart // BLOCK, BLOCK, quart).transpose(0, 2, 1, 3, 4).reshape(2, HALF, quart)
    cos_b, sin_b = np.cos(ang_b), np.sin(ang_b)
    second = np.concatenate([cos_b[:, :pair], cos_b[:, pair:], sin_b[:, 1:pair]], axis=1)
    half = lambda a: jnp.asarray(np.ascontiguousarray(a).astype(np.float32)).astype(jnp.bfloat16)
    full = lambda a: jnp.asarray(a.astype(np.float32))
    return (
        half(first), half(second), half(second.T), half(back_first),
        full(np.cos(ang_t)), full(np.sin(ang_t)),
    )


def dot(a, b):
    return jnp.dot(a, b, preferred_element_type=jnp.float32)


def kernel(
    shards, chs, rows, block,
    sig_hbm, gate_hbm, cot_hbm, gain_hbm, taps_hbm, first_hbm, second_hbm, under_hbm, back_hbm, twc_hbm, tws_hbm,
    out_ref, ggate_ref, gsig_ref, gtaps_ref,
    sig, gate, cot, gain, taps, first, second, under, back, twc, tws,
    flat, send, recv, hsend, hgrid, spec, both, stack, ysend, yrecv, tparts, tsend, trecv,
    load_sem, send_sem, recv_sem, share_send, share_recv, total_send, total_recv, ready,
):
    me = lax.axis_index("ctx")
    ch = lax.axis_index("ch")
    own = shards // chs
    tiles = N2 // 128
    quarter = shards // tiles
    hi, lo = ch // tiles, lax.rem(ch, tiles)

    loads = [
        pltpu.make_async_copy(src, dst, load_sem.at[i])
        for i, (src, dst) in enumerate(
            [(taps_hbm, taps), (sig_hbm, sig), (gate_hbm, gate), (cot_hbm, cot), (first_hbm, first),
             (twc_hbm, twc), (tws_hbm, tws), (second_hbm, second), (under_hbm, under), (back_hbm, back), (gain_hbm, gain)]
        )
    ]
    for load in loads:
        load.start()

    barrier = pltpu.get_barrier_semaphore()

    def greet_ctx(step, carry):
        pl.semaphore_signal(barrier, inc=1, device_id={"ctx": lax.rem(me + step, shards)}, device_id_type=MESH)
        return carry

    lax.fori_loop(1, shards, greet_ctx, 0)

    def is_self(peer_ctx, peer_ch):
        return jnp.logical_and(peer_ctx == me, peer_ch == ch)

    owner = me // own

    def source(at):
        return own * ch + at % own, at // own * tiles + me // quarter

    def signal(sem, condition, device):
        @pl.when(condition)
        def _():
            pl.semaphore_signal(sem, inc=1, device_id=device, device_id_type=MESH)

    for step in range(1, tiles):
        peer = lax.rem(lo + step, tiles)
        signal(barrier, peer > lo, {"ch": hi * tiles + peer})
    for at in range(quarter):
        peer_ctx, peer_ch = source(at)
        signal(barrier, peer_ch > ch, {"ctx": peer_ctx, "ch": peer_ch})
        signal(barrier, owner > ch, {"ctx": lo * quarter + at, "ch": owner})
    awaited = shards - 1 + lo + jnp.where(owner < ch, quarter, 0)
    for at in range(0, quarter, own):
        awaited = awaited + jnp.where(source(at)[1] < ch, own, 0)

    def answer():
        for step in range(1, tiles):
            peer = lax.rem(lo + step, tiles)
            signal(ready.at[0], peer < lo, {"ch": hi * tiles + peer})
        for at in range(quarter):
            peer_ctx, peer_ch = source(at)
            signal(ready.at[1], peer_ch < ch, {"ctx": peer_ctx, "ch": peer_ch})

    def place(row):
        return row // 2 + lax.rem(row, 2) * (rows // 2)

    def spread(which, value_at):
        def one(row, carry):
            for lane in range(N2 // 128):
                cols = pl.ds(pl.multiple_of(row * N2 + lane * 128, 128), 128)
                flat[lane, pl.ds(place(row), shards, stride=rows), :] = value_at(cols)
            return carry

        lax.fori_loop(0, rows, one, 0, unroll=8)

        def cast(at, carry):
            here = pl.ds(pl.multiple_of(at * rows, rows), rows)
            for lane in range(N2 // 128):
                send[which, at, :, lane * 128 : (lane + 1) * 128] = flat[lane, here, :].astype(jnp.bfloat16)
            return carry

        lax.fori_loop(0, shards, cast, 0, unroll=4)

    def remote(src, dst, which, device):
        return pltpu.make_async_remote_copy(
            src_ref=src, dst_ref=dst, send_sem=send_sem.at[which], recv_sem=recv_sem.at[which],
            device_id=device, device_id_type=MESH,
        )

    def peer_of(step):
        return lax.rem(me + step, shards)

    def each(first, last, action):
        def one(step, carry):
            action(step)
            return carry

        lax.fori_loop(first, last, one, 0, unroll=True)

    def exchange(which, src, dst):
        def one(step):
            peer = peer_of(step)
            remote(src.at[peer], dst.at[me], which, {"ctx": peer}).start()

        each(1, shards, one)
        pltpu.make_async_copy(src.at[me], dst.at[me], recv_sem.at[which]).start()

    def arrive(which, dst):
        pltpu.make_async_copy(dst, dst, recv_sem.at[which]).wait()

    def drain(which, src):
        sent = src.at[1:shards]
        pltpu.make_async_copy(sent, sent, send_sem.at[which]).wait()

    quart, pair = HALF // 2, N2 // 2
    edge = lax.broadcasted_iota(jnp.int32, (block, pair), 1) == 0

    def forward(which, load_grid):
        for at in range(quart // block):
            here = slice(at * block, (at + 1) * block)
            there = slice(quart + at * block, quart + (at + 1) * block)
            even, odd = load_grid()
            twin = slice(2 * at * block, 2 * (at + 1) * block)
            of_even, of_odd = dot(first[0, twin, :], even), dot(first[1, twin, :], odd)
            e_re, e_im, o_re, o_im = of_even[:block], of_even[block:], of_odd[:block], of_odd[block:]
            for part, rows_at, re, im in (
                (0, here, e_re + o_re, e_im + o_im), (1, there, e_re - o_re, o_im - e_im)
            ):
                cos, sin = twc[rows_at, :], tws[rows_at, :]
                both[at, part] = (re * cos + im * sin).astype(jnp.bfloat16)
                both[at, 2 + part] = (im * cos - re * sin).astype(jnp.bfloat16)
            summed = dot(both[at].reshape(4 * block, N2), second[...]).reshape(4, block, N2)
            for part, rows_at in ((0, here), (1, there)):
                r_c, r_s = summed[part][:, :pair], summed[part][:, pair:]
                i_c, i_s = summed[2 + part][:, :pair], summed[2 + part][:, pair:]
                spec[which, 0, rows_at, :pair] = jnp.where(edge, r_c, r_c + i_s)
                spec[which, 0, rows_at, pair:] = jnp.where(edge, r_s, r_c - i_s)
                spec[which, 1, rows_at, :pair] = jnp.where(edge, i_c, i_c - r_s)
                spec[which, 1, rows_at, pair:] = jnp.where(edge, i_s, i_c + r_s)

    def product(left, right, conj, rows_at, cols):
        l_re, l_im = spec[left, 0, rows_at, cols], spec[left, 1, rows_at, cols]
        r_re, r_im = spec[right, 0, rows_at, cols], spec[right, 1, rows_at, cols]
        if conj:
            return l_re * r_re + l_im * r_im, l_im * r_re - l_re * r_im
        return l_re * r_re - l_im * r_im, l_re * r_im + l_im * r_re

    def inverse(slot, left, right, conj):
        for at in range(quart // block):
            here = slice(at * block, (at + 1) * block)
            there = slice(quart + at * block, quart + (at + 1) * block)
            for part, rows_at in ((0, here), (1, there)):
                lo_re, lo_im = product(left, right, conj, rows_at, slice(0, pair))
                hi_re, hi_im = product(left, right, conj, rows_at, slice(pair, N2))
                both[at, part, :, :pair] = jnp.where(edge, lo_re, lo_re + hi_re).astype(jnp.bfloat16)
                both[at, part, :, pair:] = jnp.where(edge, hi_re, hi_im - lo_im).astype(jnp.bfloat16)
                both[at, 2 + part, :, :pair] = jnp.where(edge, lo_im, lo_im + hi_im).astype(jnp.bfloat16)
                both[at, 2 + part, :, pair:] = jnp.where(edge, hi_im, lo_re - hi_re).astype(jnp.bfloat16)
            summed = dot(both[at].reshape(4 * block, N2), under[...]).reshape(4, block, N2)
            twisted = []
            for part, rows_at in ((0, here), (1, there)):
                cos, sin = twc[rows_at, :], tws[rows_at, :]
                re, im = summed[part], summed[2 + part]
                twisted.append((re * cos - im * sin, re * sin + im * cos))
            (lo_re, lo_im), (hi_re, hi_im) = twisted
            stack[0, here, :] = (lo_re + hi_re).astype(jnp.bfloat16)
            stack[0, there, :] = (lo_im - hi_im).astype(jnp.bfloat16)
            stack[1, here, :] = (lo_re - hi_re).astype(jnp.bfloat16)
            stack[1, there, :] = (lo_im + hi_im).astype(jnp.bfloat16)
        for odd in range(2):
            value = dot(back[odd], stack[odd]).astype(jnp.bfloat16)
            ysend[slot, :, odd * (rows // 2) : (odd + 1) * (rows // 2)] = value.reshape(shards, rows // 2, N2)

    def share(step):
        return lax.rem(lo + step, tiles)

    def taps_columns(at):
        peer = hi * tiles + lax.rem(lo + (1, tiles - 1)[at], tiles)
        return pltpu.make_async_remote_copy(
            src_ref=hgrid.at[at], dst_ref=hgrid.at[3 - at], send_sem=share_send.at[0, at],
            recv_sem=share_recv.at[0, at], device_id={"ch": peer}, device_id_type=MESH,
        )

    def taps_out(step):
        peer = peer_of(step)
        remote(hsend.at[:, peer], hgrid.at[0:2, me], 1, {"ctx": peer}).start()

    def tap_terms(step):
        return pltpu.make_async_remote_copy(
            src_ref=ysend.at[2, pl.ds(share(step) * quarter, quarter)], dst_ref=tparts.at[step],
            send_sem=share_send.at[1, step], recv_sem=share_recv.at[1, step],
            device_id={"ch": hi * tiles + share(step)}, device_id_type=MESH,
        )

    def tap_term(step, at):
        return pltpu.make_async_remote_copy(
            src_ref=ysend.at[2, share(step) * quarter + at], dst_ref=tparts.at[step, at],
            send_sem=share_send.at[1, step], recv_sem=share_recv.at[1, step],
            device_id={"ch": hi * tiles + share(step)}, device_id_type=MESH,
        )

    loads[0].wait()

    def column(row, carry):
        for at in range(2):
            cols = pl.ds(pl.multiple_of(row * N2 + lax.rem(lo + at, tiles) * 128, 128), 128)
            flat[at, pl.ds(place(row), shards, stride=rows), :] = taps[:, cols]
        return carry

    lax.fori_loop(0, rows, column, 0, unroll=8)

    def cast_column(at, carry):
        for part in range(2):
            hsend[part, at] = flat[part, pl.ds(pl.multiple_of(at * rows, rows), rows), :].astype(jnp.bfloat16)
        return carry

    lax.fori_loop(0, shards, cast_column, 0, unroll=4)
    pl.semaphore_wait(barrier, awaited)
    each(1, shards, taps_out)
    pltpu.make_async_copy(hsend.at[:, me], hgrid.at[0:2, me], recv_sem.at[1]).start()
    loads[1].wait()
    spread(0, lambda cols: sig[:, cols].astype(jnp.float32))
    exchange(0, send.at[0], recv.at[0])
    answer()
    arrive(1, hgrid.at[0:2])

    @pl.when(lo < tiles - 1)
    def _():
        pl.semaphore_wait(ready.at[0], tiles - 1 - lo)

    for at in range(2):
        taps_columns(at).start()

    loads[2].wait()
    loads[3].wait()
    spread(1, lambda cols: gate[:, cols].astype(jnp.float32) * cot[:, cols].astype(jnp.float32))
    exchange(2, send.at[1], recv.at[1])
    for load in loads[4:]:
        load.wait()
    def arrived(which):
        return [
            recv[which, :, odd * (rows // 2) : (odd + 1) * (rows // 2), :].reshape(HALF // 2, N2) for odd in range(2)
        ]

    def arrived_taps():
        tile = lambda at, odd: hgrid[lax.rem(at + tiles - lo, tiles), :, odd * (rows // 2) : (odd + 1) * (rows // 2), :].reshape(HALF // 2, 128)
        return [jnp.concatenate([tile(at, odd) for at in range(tiles)], axis=1) for odd in range(2)]

    for at in range(2):
        taps_columns(at).wait_recv()
    forward(1, arrived_taps)
    arrive(0, recv.at[0])
    forward(0, lambda: arrived(0))
    inverse(0, 0, 1, False)
    exchange(3, ysend.at[0], yrecv.at[0])
    arrive(2, recv.at[1])
    forward(2, lambda: arrived(1))
    inverse(2, 2, 0, True)
    for at in range(quarter):
        for step in (2, 1, 3):
            tap_term(step, at).start()
    inverse(1, 2, 1, True)
    exchange(4, ysend.at[1], yrecv.at[1])

    sent = hsend.at[:, 1:shards]
    pltpu.make_async_copy(sent, sent, send_sem.at[1]).wait()
    drain(0, send.at[0])
    drain(2, send.at[1])
    for at in range(2):
        taps_columns(at).wait_send()
    def gather(slot):
        def one(at, carry):
            here = pl.ds(pl.multiple_of(at * rows, rows), rows)
            for lane in range(N2 // 128):
                flat[lane, here, :] = yrecv[slot, at, :, lane * 128 : (lane + 1) * 128].astype(jnp.float32)
            return carry

        lax.fori_loop(0, shards, one, 0, unroll=4)

    channel = lax.broadcasted_iota(jnp.int32, (shards, 128), 0)
    skip = jnp.zeros((shards, 128), jnp.float32)
    for at in range(shards):
        skip = jnp.where(channel == at, gain[at], skip)
    for step in range(1, tiles):
        tap_terms(step).wait_recv()
    slot = hi * own + lax.rem(me, own)

    def tap_total(at, device):
        return pltpu.make_async_remote_copy(
            src_ref=tsend.at[at], dst_ref=trecv.at[slot], send_sem=total_send.at[at], recv_sem=total_recv.at[slot],
            device_id=device, device_id_type=MESH,
        )

    def give(at, wait):
        peer = lo * quarter + at
        local = is_self(peer, owner)

        @pl.when(local)
        def _():
            copy = pltpu.make_async_copy(tsend.at[at], trecv.at[slot], total_recv.at[slot])
            copy.wait() if wait else copy.start()

        @pl.when(jnp.logical_not(local))
        def _():
            copy = tap_total(at, {"ctx": peer, "ch": owner})
            copy.wait_send() if wait else copy.start()

    def take(at):
        peer_ctx, peer_ch = source(at)

        @pl.when(jnp.logical_not(is_self(peer_ctx, peer_ch)))
        def _():
            pltpu.make_async_copy(tsend.at[0], trecv.at[at], total_recv.at[at]).wait()


    @pl.when(owner > ch)
    def _():
        pl.semaphore_wait(ready.at[1], quarter)

    for at in range(quarter):
        total = ysend[2, lo * quarter + at].astype(jnp.float32)
        for step in range(1, tiles):
            total = total + tparts[step, at].astype(jnp.float32)
        tsend[at] = total.astype(jnp.bfloat16)

        give(at, False)
    for step in range(1, tiles):
        tap_terms(step).wait_send()
    arrive(3, yrecv.at[0])
    gather(0)

    def finish_conv(row, carry):
        for lane in range(N2 // 128):
            cols = pl.ds(pl.multiple_of(row * N2 + lane * 128, 128), 128)
            mixed = flat[lane, pl.ds(place(row), shards, stride=rows), :] + skip * sig[:, cols].astype(jnp.float32)
            out_ref[:, cols] = (gate[:, cols].astype(jnp.float32) * mixed).astype(jnp.bfloat16)
            ggate_ref[:, cols] = (cot[:, cols].astype(jnp.float32) * mixed).astype(jnp.bfloat16)
        return carry

    lax.fori_loop(0, rows, finish_conv, 0, unroll=8)
    drain(3, ysend.at[0])
    arrive(4, yrecv.at[1])
    gather(1)

    def finish_corr(row, carry):
        for lane in range(N2 // 128):
            cols = pl.ds(pl.multiple_of(row * N2 + lane * 128, 128), 128)
            upstream = gate[:, cols].astype(jnp.float32) * cot[:, cols].astype(jnp.float32)
            corr = flat[lane, pl.ds(place(row), shards, stride=rows), :]
            gsig_ref[:, cols] = (corr + skip * upstream).astype(jnp.bfloat16)
        return carry

    lax.fori_loop(0, rows, finish_corr, 0, unroll=8)
    for at in range(quarter):
        give(at, True)
    for at in range(quarter):
        take(at)
    scale = 1.0 / math.sqrt(SEQ)
    for group in range(own):
        total = trecv[group].astype(jnp.float32)
        for at in range(own + group, quarter, own):
            total = total + trecv[at].astype(jnp.float32)
        for lane in range(N2 // 128):
            flat[lane, group * rows : (group + 1) * rows, :] = total[:, lane * 128 : (lane + 1) * 128] * scale

    def finish_taps(row, carry):
        for lane in range(N2 // 128):
            cols = pl.ds(pl.multiple_of(row * N2 + lane * 128, 128), 128)
            gtaps_ref[:, cols] = flat[lane, pl.ds(place(row), own, stride=rows), :]
        return carry

    lax.fori_loop(0, rows, finish_taps, 0, unroll=8)
    drain(4, ysend.at[1])


def emit(*refs):
    copies = [pltpu.make_async_copy(refs[at], refs[4 + at], refs[8].at[at]) for at in range(4)]
    for copy in copies:
        copy.start()
    for copy in copies:
        copy.wait()


def body(shards, chs, signal, gate, cotangent, skip_gain, filter_taps):
    channels, positions = signal.shape
    rows = positions // N2
    own = shards // chs
    block = BLOCK
    bf16, f32 = jnp.bfloat16, jnp.float32
    hbm = pl.BlockSpec(memory_space=pl.ANY)
    vmem = pl.BlockSpec(memory_space=pltpu.VMEM)
    operands = signal, gate, cotangent, skip_gain, filter_taps, *tables()
    results = pl.pallas_call(
        functools.partial(kernel, shards, chs, rows, block),
        out_shape=[jax.ShapeDtypeStruct((channels, positions), bf16)] * 3
        + [jax.ShapeDtypeStruct((own, positions), f32)],
        in_specs=[hbm] * 11,
        out_specs=[vmem] * 4,
        scratch_shapes=[
            pltpu.VMEM((channels, positions), bf16),
            pltpu.VMEM((channels, positions), bf16),
            pltpu.VMEM((channels, positions), bf16),
            pltpu.SMEM((channels,), f32),
            pltpu.VMEM((channels, positions), f32),
            pltpu.VMEM((2, HALF, HALF // 2), bf16),
            pltpu.VMEM((N2, N2), bf16),
            pltpu.VMEM((N2, N2), bf16),
            pltpu.VMEM((2, HALF // 2, HALF), bf16),
            pltpu.VMEM((HALF, N2), f32),
            pltpu.VMEM((HALF, N2), f32),
            pltpu.VMEM((N2 // 128, HALF, 128), f32),
            pltpu.VMEM((2, shards, rows, N2), bf16),
            pltpu.VMEM((2, shards, rows, N2), bf16),
            pltpu.VMEM((2, shards, rows, 128), bf16),
            pltpu.VMEM((N2 // 128, shards, rows, 128), bf16),
            pltpu.VMEM((3, 2, HALF, N2), f32),
            pltpu.VMEM((HALF // 2 // block, 4, block, N2), bf16),
            pltpu.VMEM((2, HALF, N2), bf16),
            pltpu.VMEM((3, shards, rows, N2), bf16),
            pltpu.VMEM((2, shards, rows, N2), bf16),
            pltpu.VMEM((N2 // 128, shards * 128 // N2, rows, N2), bf16),
            pltpu.VMEM((shards * 128 // N2, rows, N2), bf16),
            pltpu.VMEM((shards * 128 // N2, rows, N2), bf16),
            pltpu.SemaphoreType.DMA((11,)),
            pltpu.SemaphoreType.DMA((5,)),
            pltpu.SemaphoreType.DMA((5,)),
            pltpu.SemaphoreType.DMA((2, N2 // 128)),
            pltpu.SemaphoreType.DMA((2, N2 // 128)),
            pltpu.SemaphoreType.DMA((shards * 128 // N2,)),
            pltpu.SemaphoreType.DMA((shards * 128 // N2,)),
            pltpu.SemaphoreType.REGULAR((2,)),
        ],
        compiler_params=pltpu.CompilerParams(
            collective_id=0, has_side_effects=True, vmem_limit_bytes=48 * 1024 * 1024
        ),
    )(*[pltpu.with_memory_space_constraint(operand, pltpu.HBM) for operand in operands])
    return pl.pallas_call(
        emit,
        out_shape=[jax.ShapeDtypeStruct(result.shape, result.dtype) for result in results],
        in_specs=[hbm] * 4,
        out_specs=[hbm] * 4,
        scratch_shapes=[pltpu.SemaphoreType.DMA((4,))],
        compiler_params=pltpu.CompilerParams(vmem_limit_bytes=1024 * 1024),
    )(*results)


def solution(mesh):
    return jax.shard_map(
        functools.partial(body, mesh.shape["ctx"], mesh.shape["ch"]),
        mesh=mesh,
        in_specs=(P("ch", "ctx"), P("ch", "ctx"), P("ch", "ctx"), P("ch"), P(None, "ctx")),
        out_specs=(P("ch", "ctx"), P("ch", "ctx"), P("ch", "ctx"), P("ch", "ctx")),
        check_vma=False,
    )
```
